128 devices in a mesh: group: 2 (over z_lo), dp: 8 (over x, z_hi), space: 8 (over y, core).
Axes of the slice: x: 4, y: 4, z: 4 (z_hi: 2, z_lo: 2; z = z_hi * 2 + z_lo), core: 2. Of those that a mesh axis runs over, the one named last changes fastest.
Arguments:
- velocity: float32 [3, 320, 32, 1024], P(None, ('group', 'dp'), None, 'space'), may hold values from -6 to 6
- conv_first: bfloat16 [27, 64, 3], replicated, may hold values from -3 to 3
- conv_mid: bfloat16 [27, 64, 64], replicated, may hold values from -0.15625 to 0.15625
- conv_last: bfloat16 [6, 64], replicated, may hold values from -0.75 to 0.75
- corner_x: int32 [16, 8], replicated, may hold values from 0 to 4
- corner_z: int32 [16, 8], replicated, may hold values from 0 to 16
- corner_y: int32 [16, 8], replicated, may hold values from 0 to 112
- patch_live: int32 [16, 8], replicated, may hold values from 0 to 1, as said below
- patch_dest: int32 [16, 8], replicated, may hold values from 0 to 15, as said below
Outputs:
- velocity_next: float32 [3, 320, 32, 1024], P(None, ('group', 'dp'), None, 'space')
- filtered: float32 [3, 320, 32, 1024], P(None, ('group', 'dp'), None, 'space')
- stress: float32 [6, 320, 32, 1024], P(None, ('group', 'dp'), None, 'space')
- grad_first: float32 [27, 64, 3], replicated
- grad_mid: float32 [27, 64, 64], replicated
- grad_last: float32 [6, 64], replicated
- replica_loss: float32 [16], P(('group', 'dp'))
The draws below stay inside these ranges and needn't reach their ends.
Inputs may be any that keep to these rules, and one draw needn't show every extreme that they name: `patch_live`: each row of blocks (first index) holds exactly 2 ones. `patch_dest`: among the blocks with patch_live = 1, no replica is named more than 4 times, and some replica exactly 4 times.
All inputs are finite; a program needn't handle non-finite values.
Results may differ from the reference program's by a relative error of at most 0.0003.
Values may be sent and summed in bfloat16 or wider, within the bound.
No kernel may reach another device: no remote copies, remote signals or barrier semaphores. Data moves between devices by JAX's collectives and lax.ppermute only.
A program may use at most 64 MiB of HBM per device.

```python
import jax
import jax.numpy as jnp
from jax import lax

CH = 64
PE = 16
CX = 20
CY = 128
NZ = 32
SOLVER_STEPS = 2
FILTER_PASSES = 3
LIVE_ROW = 2
REPLICAS = 16
BLOCK_COLS = 8
NX = 320
NY = 1024


def shared_sampling(key):
    key_live, key_patch, key_replica, key_spare = jax.random.split(key, 4)
    row_total = REPLICAS
    col_total = BLOCK_COLS
    scores = jax.random.randint(key_live, (row_total, col_total), 0, 1 << 20) * col_total + jnp.arange(col_total)[None, :]
    ordering = jnp.argsort(scores, axis=1)
    live_rank = jnp.argsort(ordering, axis=1)
    live_flags = (live_rank < LIVE_ROW).astype(jnp.int32)
    live_total = row_total * LIVE_ROW
    block_size = 4 * LIVE_ROW
    position = jnp.arange(live_total)
    within = position % block_size
    sub_replica = (within >= 2 * LIVE_ROW).astype(jnp.int32) + (within >= 3 * LIVE_ROW).astype(jnp.int32) + (within >= 3 * LIVE_ROW + LIVE_ROW // 2).astype(jnp.int32)
    owner_replica = position // block_size * 4 + sub_replica
    patch_scores = jax.random.randint(key_patch, (live_total,), 0, 1 << 20) * live_total + position
    patch_order = jnp.argsort(patch_scores)
    replica_scores = jax.random.randint(key_replica, (row_total,), 0, 1 << 20) * row_total + jnp.arange(row_total)
    replica_order = jnp.argsort(replica_scores)
    live_dest = replica_order[owner_replica[patch_order]]
    flat_live = live_flags.reshape(-1)
    live_number = jnp.clip(jnp.cumsum(flat_live) - 1, 0, live_total - 1)
    spare_dest = jax.random.randint(key_spare, (row_total * col_total,), 0, row_total)
    dest_table = jnp.where(flat_live == 1, live_dest[live_number], spare_dest).reshape(row_total, col_total).astype(jnp.int32)
    return (live_flags, dest_table)


def draw_patch_live(key, part):
    return shared_sampling(key)[0]


def draw_patch_dest(key, part):
    return shared_sampling(key)[1]


def set_ends(drawn, stream_key, smallest, high):
    shape = drawn.shape
    spot = [jax.random.randint(jax.random.fold_in(stream_key, axis), (), 0, shape[axis]) for axis in range(len(shape))]
    drawn = drawn.at[tuple(spot)].set(smallest)
    longest = shape.index(max(shape))
    spot[longest] = (spot[longest] + 1) % shape[longest]
    return drawn.at[tuple(spot)].set(high)


def block_scale(own_key, shape, cuts, low, largest):
    def one(dim, blocks):
        draws = jax.random.uniform(jax.random.fold_in(jax.random.fold_in(own_key, 6), dim), (blocks,), jnp.float32, low / len(cuts), largest / len(cuts))
        return jnp.repeat(jnp.exp(draws), shape[dim] // blocks).reshape((-1,) + (1,) * (len(shape) - dim - 1))

    factor_of = one(*cuts[0])
    for cut in cuts[1:]:
        factor_of = factor_of * one(*cut)
    return factor_of


def gaussian(key, shape, spread, most, pieces=(), kind=jnp.bfloat16):
    factor_of = block_scale(key, shape, pieces, -0.22, 0.18) if pieces else 1.0
    array = jax.random.normal(key, shape, jnp.float32) * spread * factor_of
    return jnp.minimum(jnp.maximum(array, -most), most).astype(kind)


def setup_inputs(seed: int = 0) -> dict:
    key_of = jax.random.split(jax.random.key(seed), 10)
    return {
        "velocity": gaussian(key_of[0], (3, NX, NZ, NY), 1.0, 6.0, ((1, 16), (3, 8)), jnp.float32),
        "conv_first": gaussian(key_of[1], (27, CH, 3), 4 ** -0.5, 3.0),
        "conv_mid": gaussian(key_of[2], (27, CH, CH), (27 * CH) ** -0.5, 0.15625),
        "conv_last": gaussian(key_of[3], (6, CH), CH ** -0.5, 0.75),
        "corner_x": set_ends(jax.random.randint(key_of[4], (REPLICAS, BLOCK_COLS), 0, CX - PE + 1), jax.random.fold_in(key_of[4], 1), 0, CX - PE).astype(jnp.int32),
        "corner_z": set_ends(jax.random.randint(key_of[5], (REPLICAS, BLOCK_COLS), 0, NZ - PE + 1), jax.random.fold_in(key_of[5], 1), 0, NZ - PE).astype(jnp.int32),
        "corner_y": set_ends(jax.random.randint(key_of[6], (REPLICAS, BLOCK_COLS), 0, CY - PE + 1), jax.random.fold_in(key_of[6], 1), 0, CY - PE).astype(jnp.int32),
        "patch_live": draw_patch_live(jax.random.fold_in(key_of[9], 71), 0),
        "patch_dest": draw_patch_dest(jax.random.fold_in(key_of[9], 71), 0),
    }


time_step = 0.05
viscosity = 0.1

def products(field):
    return jnp.stack([field[0] * field[0], field[1] * field[1], field[2] * field[2], field[0] * field[1], field[0] * field[2], field[1] * field[2]])

def combine(middle, x_plus, x_minus, y_plus, y_minus, z_plus, z_minus):
    advect = middle[0:1] * ((x_plus - x_minus) * 0.5) + middle[1:2] * ((y_plus - y_minus) * 0.5) + middle[2:3] * ((z_plus - z_minus) * 0.5)
    laplace = x_plus + x_minus + y_plus + y_minus + z_plus + z_minus - 6.0 * middle
    return middle + time_step * (viscosity * laplace - advect)

def advance_roll(velocity_now):
    padded = jnp.pad(velocity_now, ((0, 0), (0, 0), (1, 1), (0, 0)))
    return combine(velocity_now, jnp.roll(velocity_now, -1, axis=1), jnp.roll(velocity_now, 1, axis=1), jnp.roll(velocity_now, -1, axis=3), jnp.roll(velocity_now, 1, axis=3), padded[:, :, 2:], padded[:, :, :-2])

def smooth_roll(fields):
    along_x = 0.25 * jnp.roll(fields, 1, axis=1) + 0.5 * fields + 0.25 * jnp.roll(fields, -1, axis=1)
    return 0.25 * jnp.roll(along_x, 1, axis=3) + 0.5 * along_x + 0.25 * jnp.roll(along_x, -1, axis=3)

def live_slots(live_flags, dest_table):
    live_rank = (jnp.cumsum(live_flags, axis=1) - 1).astype(jnp.int32)
    slot_index = jnp.arange(LIVE_ROW, dtype=jnp.int32)
    slot_hit = (live_flags[:, None, :] == 1) & (live_rank[:, None, :] == slot_index[None, :, None])
    column = jnp.arange(live_flags.shape[1], dtype=jnp.int32)
    owner_col = lax.optimization_barrier(jnp.sum(jnp.where(slot_hit, column[None, None, :], 0), axis=2)).astype(jnp.int32)
    target_row = lax.optimization_barrier(jnp.sum(jnp.where(slot_hit, dest_table[:, None, :], 0), axis=2)).astype(jnp.int32)
    return (owner_col, target_row)

def conv_apply(activation, kernel):
    return lax.conv_general_dilated(activation[None], kernel, (1, 1, 1), [(1, 1), (1, 1), (1, 1)], precision=lax.Precision.HIGHEST)[0]

def to_kernel(weight):
    return weight.astype(jnp.float32).reshape(3, 3, 3, weight.shape[1], weight.shape[2]).transpose(3, 4, 0, 1, 2)

def from_kernel(kernel):
    return kernel.transpose(2, 3, 4, 0, 1).reshape(27, kernel.shape[0], kernel.shape[1])

def rounded(value):
    return lax.optimization_barrier(value.astype(jnp.bfloat16)).astype(jnp.float32)

def silu_slope(value):
    sigmoid = jax.nn.sigmoid(value)
    return sigmoid * (1.0 + value * (1.0 - sigmoid))

def reference(velocity, conv_first, conv_mid, conv_last, corner_x, corner_z, corner_y, patch_live, patch_dest):
    velocity_now = velocity
    for repeat in range(SOLVER_STEPS):
        velocity_now = advance_roll(velocity_now)
    fields = jnp.concatenate([velocity_now, products(velocity_now)], axis=0)
    for repeat in range(FILTER_PASSES):
        fields = smooth_roll(fields)
    filtered = fields[0:3]
    stress = fields[3:9] - products(filtered)
    stacked = jnp.concatenate([filtered, stress], axis=0)
    owner_col, target_row = live_slots(patch_live, patch_dest)
    row_index = jnp.repeat(jnp.arange(REPLICAS, dtype=jnp.int32), LIVE_ROW)
    owner_flat = owner_col.reshape(-1)
    target_flat = target_row.reshape(-1)
    start_x = (row_index * CX + corner_x[row_index, owner_flat]).astype(jnp.int32)
    start_z = corner_z[row_index, owner_flat].astype(jnp.int32)
    start_y = (owner_flat * CY + corner_y[row_index, owner_flat]).astype(jnp.int32)
    kernel_first = to_kernel(conv_first)
    kernel_mid = to_kernel(conv_mid)
    last_weight = conv_last.astype(jnp.float32)
    grad_scale = 2.0 / (PE ** 3 * REPLICAS * LIVE_ROW)
    zero_index = jnp.zeros((), jnp.int32)

    def train_one(carry, item):
        begin_x, begin_z, begin_y, target_index = item
        patch_block = rounded(lax.dynamic_slice(stacked, (zero_index, begin_x, begin_z, begin_y), (9, PE, PE, PE)))
        inputs = patch_block[0:3]
        target = patch_block[3:9]
        pre_first = conv_apply(inputs, kernel_first)
        hidden_first = rounded(jax.nn.silu(pre_first))
        pre_mid = conv_apply(hidden_first, kernel_mid)
        hidden_mid = rounded(jax.nn.silu(pre_mid))
        predicted = jnp.einsum('oc,cxzy->oxzy', last_weight, hidden_mid, precision=lax.Precision.HIGHEST)
        mismatch = predicted - target
        squared = jnp.sum(mismatch * mismatch) / PE ** 3
        grad_pred = rounded(mismatch * grad_scale)
        grad_last = jnp.einsum('oxzy,cxzy->oc', grad_pred, hidden_mid, precision=lax.Precision.HIGHEST)
        grad_hidden = jnp.einsum('oc,oxzy->cxzy', last_weight, grad_pred, precision=lax.Precision.HIGHEST)
        grad_pre_mid = rounded(grad_hidden * silu_slope(pre_mid))
        unused, pullback_mid = jax.vjp(conv_apply, hidden_first, kernel_mid)
        grad_first_hidden, grad_kernel_mid = pullback_mid(grad_pre_mid)
        grad_pre_first = rounded(grad_first_hidden * silu_slope(pre_first))

        def first_layer(kernel):
            return conv_apply(inputs, kernel)
        unused, pullback_first = jax.vjp(first_layer, kernel_first)
        grad_kernel_first = pullback_first(grad_pre_first)[0]
        loss_add = (jnp.arange(REPLICAS, dtype=jnp.int32) == target_index).astype(jnp.float32) * (squared / LIVE_ROW)
        updated = (carry[0] + from_kernel(grad_kernel_first), carry[1] + from_kernel(grad_kernel_mid), carry[2] + grad_last, carry[3] + loss_add)
        return (updated, None)
    initial = (jnp.zeros((27, CH, 3), jnp.float32), jnp.zeros((27, CH, CH), jnp.float32), jnp.zeros((6, CH), jnp.float32), jnp.zeros((REPLICAS,), jnp.float32))
    summed, unused = lax.scan(train_one, initial, (start_x, start_z, start_y, target_flat))
    return (velocity_now, filtered, stress, summed[0], summed[1], summed[2], summed[3])
```

```python
import functools

import jax
import jax.numpy as jnp
from jax import lax
from jax.experimental import pallas as pl
from jax.experimental.pallas import tpu as pltpu
from jax.sharding import PartitionSpec as P

PE = 16
CELLS = PE * PE
LIVE_ROW = 2
HALO = 5
LANES = 128
ROWS = ("group", "dp")
EVERY = ("group", "dp", "space")
VIEWS = [(dz, dy) for dz in (-1, 0, 1) for dy in (-1, 0, 1)]
F32 = jnp.float32
BF16 = jnp.bfloat16


def lane_of(shape):
    return lax.broadcasted_iota(jnp.int32, shape, len(shape) - 1)


def roll(value, shift, axis=1):
    size = value.shape[axis]
    if isinstance(shift, int):
        shift = shift % size
        if shift == 0:
            return value
    return pltpu.roll(value, shift, axis)


def pack_kernel(vel, lo, hi):
    count = vel.shape[1]
    lane = lane_of((vel.shape[2], LANES))
    for c in range(3):
        first = jnp.zeros(lane.shape, F32)
        last = jnp.zeros(lane.shape, F32)
        for r in range(count):
            here = (lane >= HALO * r) & (lane < HALO * r + HALO)
            row = vel[c, r]
            first = jnp.where(here, roll(row, HALO * r), first)
            last = jnp.where(here, roll(row, HALO * r + HALO), last)
        lo[c] = first
        hi[c] = last


def corner_kernel(left, right, out):
    lane = lane_of((left.shape[1], LANES))
    wide = HALO * HALO
    for c in range(3):
        lhs = left[c]
        rhs = right[c]
        value = jnp.where((lane >= wide) & (lane < 2 * wide), roll(rhs, wide), lhs)
        out[c] = jnp.where((lane >= 2 * wide) & (lane < 3 * wide), roll(rhs, -wide), value)


def products(a, b, c):
    return [a * a, b * b, c * c, a * b, a * c, b * c]


def slab_kernel(vel, xlo, xhi, left, right, below, above, nxt, filt, stress, wa, wb):
    count = vel.shape[1]
    levels = vel.shape[2]
    lane = lane_of((levels, LANES))
    wide = HALO * HALO
    for c in range(3):
        for r in range(count + 2 * HALO):
            if r < HALO:
                main = xlo[c, r]
                lsrc, lat = below[c], 3 * wide + HALO * r
                rsrc, rat = below[c], 2 * wide + HALO * r
            elif r < count + HALO:
                q = r - HALO
                main = vel[c, q]
                lsrc, lat = left[c], HALO * q
                rsrc, rat = right[c], HALO * q
            else:
                q = r - HALO - count
                main = xhi[c, q]
                lsrc, lat = above[c], HALO * q
                rsrc, rat = above[c], wide + HALO * q
            wa[c, r, :, 0:LANES] = main
            wa[c, r, :, LANES:] = jnp.where(
                lane < 64, roll(rsrc, -rat), roll(lsrc, LANES - HALO - lat)
            )
    level = lax.broadcasted_iota(jnp.int32, (levels, 2 * LANES), 0)

    def step(src, dst, n):
        def body(r, carry):
            mids = [src[c, r + 1] for c in range(3)]
            for c in range(3):
                mid = mids[c]
                xp = src[c, r + 2]
                xm = src[c, r]
                yp = roll(mid, -1)
                ym = roll(mid, 1)
                zp = jnp.where(level == levels - 1, 0.0, roll(mid, -1, 0))
                zm = jnp.where(level == 0, 0.0, roll(mid, 1, 0))
                adv = mids[0] * (xp - xm) + mids[1] * (yp - ym) + mids[2] * (zp - zm)
                lap = (xp + xm) + (yp + ym) + (zp + zm) - 6.0 * mid
                dst[c, r] = mid + (0.005 * lap - 0.025 * adv)
            return carry

        lax.fori_loop(0, n, body, 0)

    step(wa, wb, count + 2 * HALO - 2)
    step(wb, wa, count + 2 * HALO - 4)
    for c in range(3):
        nxt[c] = wa[c, 3 : 3 + count, :, 0:LANES]
    tile = 8
    lanes = lane_of((tile, LANES))

    def along_x(rows):
        return (
            20.0 * rows[3]
            + 15.0 * (rows[2] + rows[4])
            + 6.0 * (rows[1] + rows[5])
            + (rows[0] + rows[6])
        )

    def along_y(f):
        m, e = f[:, :LANES], f[:, LANES:]
        rm, re = roll(m, -1), roll(e, -1)
        up_m = jnp.where(lanes == LANES - 1, re, rm)
        up_e = jnp.where(lanes == LANES - 1, rm, re)
        rm, re = roll(m, 1), roll(e, 1)
        dn_m = jnp.where(lanes == 0, re, rm)
        dn_e = jnp.where(lanes == 0, rm, re)
        far_up = jnp.where(
            lanes >= LANES - 2, roll(6.0 * e + up_e, -2), roll(6.0 * m + up_m, -2)
        )
        far_dn = jnp.where(lanes < 2, roll(6.0 * e + dn_e, 2), roll(6.0 * m + dn_m, 2))
        return (20.0 * m + 15.0 * (up_m + dn_m) + (far_up + far_dn)) * (1.0 / 4096.0)

    def filter_row(r, carry):
        for t in range(levels // tile):
            zs = slice(t * tile, (t + 1) * tile)
            rows = [[wa[c, r + k, zs, :] for k in range(7)] for c in range(3)]
            done = [along_y(along_x(rows[c])) for c in range(3)]
            for c in range(3):
                filt[c, r, zs, :] = done[c]
            small = products(*done)
            pairs = [(0, 0), (1, 1), (2, 2), (0, 1), (0, 2), (1, 2)]
            for i, (a, b) in enumerate(pairs):
                big = along_y(along_x([rows[a][k] * rows[b][k] for k in range(7)]))
                stress[i, r, zs, :] = big - small[i]
        return carry

    lax.fori_loop(0, count, filter_row, 0)


def views_of(halves, width):
    lane = lane_of(halves[0].shape)
    column = lane & (PE - 1)
    by_y = {
        0: halves,
        1: [jnp.where(column == PE - 1, 0.0, roll(h, -1)) for h in halves],
        -1: [jnp.where(column == 0, 0.0, roll(h, 1)) for h in halves],
    }
    out = []
    for dz, dy in VIEWS:
        a, b = by_y[dy]
        if dz == 0:
            out.append((a, b))
        elif dz == 1:
            ra, rb = roll(a, -PE), roll(b, -PE)
            inner = lane < LANES - PE
            out.append((jnp.where(inner, ra, rb), jnp.where(inner, rb, 0.0)))
        else:
            ra, rb = roll(a, PE), roll(b, PE)
            inner = lane >= PE
            out.append((jnp.where(inner, ra, 0.0), jnp.where(inner, rb, ra)))
    return out


def silu_parts(value):
    sigmoid = 1.0 / (1.0 + jnp.exp(-value))
    return value * sigmoid, sigmoid * (1.0 + value * (1.0 - sigmoid))


def dot_nn(a, b):
    return lax.dot_general(a, b, (((1,), (0,)), ((), ())), preferred_element_type=F32)


def dot_nt(a, b):
    return lax.dot_general(a, b, (((1,), (1,)), ((), ())), preferred_element_type=F32)


def cols(x, offset=0):
    return pl.ds(pl.multiple_of((x + offset) * CELLS, CELLS), CELLS)


def half_cols(x, half):
    return pl.ds(pl.multiple_of(x * CELLS + half * LANES, LANES), LANES)


def train_kernel(
    grad_scale, where, filt, stress, w1, w2, w2b, wl, wlt, out, src, tgt, xv, vv, yy, s1, s2, gs, acc
):
    live = where[0]

    @pl.when(live == 0)
    def _():
        out[...] = jnp.zeros(out.shape, F32)

    @pl.when(live != 0)
    def _():
        bx, bz, by, dest = where[1], where[2], where[3], where[4]
        src[...] = jnp.zeros(src.shape, F32)
        tgt[...] = jnp.zeros(tgt.shape, F32)
        lane16 = lane_of((PE, LANES)) // PE
        for f in range(9):
            ref, g = (filt, f) if f < 3 else (stress, f - 3)
            halves = [jnp.zeros((PE, LANES), F32)] * 2
            for z in range(PE):
                piece = ref[g, pl.ds(bx * 32 + bz + z, PE, stride=32), :]
                moved = roll(piece, lax.rem(PE * z - by + 2 * LANES, LANES))
                halves[z // 8] = jnp.where(lane16 == z % 8, moved, halves[z // 8])
            to = src if f < 3 else tgt
            for x in range(PE):
                for half in range(2):
                    at = x * CELLS + half * LANES
                    to[g : g + 1, at : at + LANES] = halves[half][x : x + 1, :]
        edge = jnp.zeros((yy.shape[0], CELLS), F32)
        yy[:, 0:CELLS] = edge
        yy[:, (PE + 1) * CELLS :] = edge

        def forward(x):
            return (
                yy[0:64, cols(x)] + yy[64:128, cols(x, 1)] + yy[128:192, cols(x, 2)]
            )

        def backward(x):
            return (
                yy[0:64, cols(x, 2)] + yy[64:128, cols(x, 1)] + yy[128:192, cols(x)]
            )

        def store_views(to, x, values, height):
            for k, pair in enumerate(views_of([values[:, :LANES], values[:, LANES:]], height)):
                for half in range(2):
                    to[height * k : height * (k + 1), half_cols(x, half)] = pair[half].astype(BF16)

        def input_views(x, carry):
            value = src[:, cols(x)].astype(BF16).astype(F32)
            for k, pair in enumerate(views_of([value[:, :LANES], value[:, LANES:]], 8)):
                for half in range(2):
                    xv[8 * k : 8 * (k + 1), half_cols(x, half)] = pair[half]
            return carry

        lax.fori_loop(0, PE, input_views, 0)

        def conv_a(x, carry):
            yy[:, cols(x, 1)] = dot_nn(w1[...], xv[:, cols(x)].astype(BF16))
            return carry

        lax.fori_loop(0, PE, conv_a, 0, unroll=2)

        def hidden_a(x, carry):
            hidden, slope = silu_parts(forward(x))
            s1[:, cols(x)] = slope
            store_views(vv, x, hidden.astype(BF16).astype(F32), 64)
            return carry

        lax.fori_loop(0, PE, hidden_a, 0)

        def conv_b(x, carry):
            yy[:, cols(x, 1)] = dot_nn(w2[...], vv[:, cols(x)])
            return carry

        lax.fori_loop(0, PE, conv_b, 0, unroll=2)

        none = jnp.zeros((64, CELLS), BF16)
        gs[0:64, (PE - 1) * CELLS :] = none
        gs[128:192, 0:CELLS] = none

        def last(x, carry):
            total, grad_last = carry
            hidden, slope = silu_parts(forward(x))
            hidden = hidden.astype(BF16)
            goal = tgt[:, cols(x)].astype(BF16).astype(F32)
            miss = dot_nn(wl[...], hidden) - goal
            total = total + miss * miss
            grad_pred = (miss * grad_scale).astype(BF16)
            grad_last = grad_last + dot_nt(grad_pred, hidden)
            grad = (dot_nn(wlt[...], grad_pred) * slope).astype(BF16)
            s2[:, cols(x)] = grad

            gs[64:128, cols(x)] = grad

            @pl.when(x > 0)
            def _():
                gs[0:64, cols(x, -1)] = grad

            @pl.when(x < PE - 1)
            def _():
                gs[128:192, cols(x, 1)] = grad

            return total, grad_last

        zero = (jnp.zeros((8, CELLS), F32), jnp.zeros((8, 64), F32))
        total, grad_last = lax.fori_loop(0, PE, last, zero)

        acc[...] = jnp.zeros(acc.shape, F32)
        span = 4 * CELLS

        def weight_b(i, carry):
            at = pl.ds(pl.multiple_of(i * span, span), span)
            acc[...] += dot_nt(gs[:, at], vv[:, at])
            return carry

        lax.fori_loop(0, PE * CELLS // span, weight_b, 0)

        def grad_views(x, carry):
            store_views(vv, x, s2[:, cols(x)].astype(F32), 64)
            return carry

        lax.fori_loop(0, PE, grad_views, 0)

        def conv_c(x, carry):
            yy[:, cols(x, 1)] = dot_nn(w2b[...], vv[:, cols(x)])
            return carry

        lax.fori_loop(0, PE, conv_c, 0, unroll=2)

        def first(x, carry):
            grad = (backward(x) * s1[:, cols(x)]).astype(BF16)
            gs[64:128, cols(x)] = grad

            @pl.when(x > 0)
            def _():
                gs[0:64, cols(x, -1)] = grad

            @pl.when(x < PE - 1)
            def _():
                gs[128:192, cols(x, 1)] = grad

            return carry

        lax.fori_loop(0, PE, first, 0)
        grad_first = dot_nt(xv[...].astype(BF16), gs[...])

        for i in range(24):
            for j in range(4):
                out[4 * i + j] = acc[8 * i : 8 * i + 8, LANES * j : LANES * (j + 1)]
        for i in range(12):
            out[96 + i] = jnp.concatenate(
                [acc[8 * i : 8 * i + 8, 512:576], acc[8 * i + 96 : 8 * i + 104, 512:576]], axis=1
            )
        for i in range(9):
            out[108 + i] = grad_first[8 * i : 8 * i + 8, 0:LANES]
        for i in range(5):
            j = min(i + 5, 8)
            out[117 + i] = jnp.concatenate(
                [grad_first[8 * i : 8 * i + 8, 128:192], grad_first[8 * j : 8 * j + 8, 128:192]],
                axis=1,
            )
        loss = jnp.sum(total) * (1.0 / (PE**3 * LIVE_ROW))
        corner = lane_of((8, LANES))
        deep = lax.broadcasted_iota(jnp.int32, (8, LANES), 0)
        padded = jnp.concatenate([grad_last, jnp.zeros((8, 64), F32)], axis=1)
        out[122] = jnp.where((deep == 7) & (corner == 64 + dest), loss, padded)
        for i in range(123, 128):
            out[i] = jnp.zeros((8, LANES), F32)


def unpack_kernel(where, parts, first, mid, last, loss):
    for dx in range(3):
        for t in range(8):
            i = 8 * dx + t
            for k in range(9):
                if k < 8:
                    block, half = parts[4 * i + k // 2], k % 2
                else:
                    block, half = parts[96 + i % 12], i // 12
                mid[9 * dx + k, 8 * t : 8 * t + 8, :] = block[:, 64 * half : 64 * half + 64]
    for k in range(9):
        tail = parts[117 + k % 5]
        half = k // 5
        wide = jnp.concatenate([parts[108 + k], tail[:, 64 * half : 64 * half + 64]], axis=1)
        turned = wide.T
        for dx in range(3):
            first[9 * dx + k] = turned[64 * dx : 64 * dx + 64, 0:3]
    final = parts[122]
    last[...] = final[0:6, 0:64]
    corner = lane_of((8, LANES))
    deep = lax.broadcasted_iota(jnp.int32, (8, LANES), 0)
    mine = (deep == 7) & (corner == 64 + where[5])
    loss[0] = jnp.sum(jnp.where(mine, final, 0.0))


def table_entry(table, row, col):
    hit = (jnp.arange(table.shape[0])[:, None] == row) & (jnp.arange(table.shape[1])[None] == col)
    return jnp.sum(jnp.where(hit, table, 0))


VMEM = pl.BlockSpec(memory_space=pltpu.VMEM)
SMEM = pl.BlockSpec(memory_space=pltpu.SMEM)


def params(mib):
    return pltpu.CompilerParams(vmem_limit_bytes=mib * 1024 * 1024)


def train_call(where, filt, stress, conv_first, conv_mid, conv_last, row_count):
    count, levels = filt.shape[1], filt.shape[2]
    w1 = conv_first.reshape(3, 9, 64, 3).transpose(0, 2, 1, 3)
    w1 = jnp.pad(w1, ((0, 0), (0, 0), (0, 0), (0, 5))).reshape(192, 72)
    by_k = conv_mid.reshape(3, 9, 64, 64)
    w2 = by_k.transpose(0, 2, 1, 3).reshape(192, 576)
    w2b = by_k[:, ::-1].transpose(0, 3, 1, 2).reshape(192, 576)
    wl = jnp.pad(conv_last, ((0, 2), (0, 0)))
    grad_scale = 2.0 / (PE**3 * row_count * LIVE_ROW)
    whole = PE * CELLS
    return pl.pallas_call(
        functools.partial(train_kernel, grad_scale),
        out_shape=jax.ShapeDtypeStruct((128, 8, LANES), F32),
        in_specs=[SMEM] + [VMEM] * 7,
        out_specs=VMEM,
        scratch_shapes=[
            pltpu.VMEM((8, whole), F32),
            pltpu.VMEM((8, whole), F32),
            pltpu.VMEM((72, whole), F32),
            pltpu.VMEM((576, whole), BF16),
            pltpu.VMEM((192, whole + 2 * CELLS), F32),
            pltpu.VMEM((64, whole), F32),
            pltpu.VMEM((64, whole), BF16),
            pltpu.VMEM((192, whole), BF16),
            pltpu.VMEM((192, 576), F32),
        ],
        compiler_params=params(48),
    )(
        where,
        filt.reshape(3, count * levels, LANES),
        stress.reshape(6, count * levels, LANES),
        w1,
        w2,
        w2b,
        wl,
        wl.T,
    )


def local(
    velocity, conv_first, conv_mid, conv_last, corner_x, corner_z, corner_y, patch_live, patch_dest
):
    row_count = patch_live.shape[0]
    my_row = lax.axis_index("group") * lax.axis_size("dp") + lax.axis_index("dp")
    my_col = lax.axis_index("space")
    _, count, levels, _ = velocity.shape
    strip = jax.ShapeDtypeStruct((3, levels, LANES), F32)
    up_row = [(i, (i + 1) % row_count) for i in range(row_count)]
    down_row = [(j, i) for i, j in up_row]
    cols_n = lax.axis_size("space")
    up_col = [(i, (i + 1) % cols_n) for i in range(cols_n)]
    down_col = [(j, i) for i, j in up_col]

    lo, hi = pl.pallas_call(
        pack_kernel, out_shape=(strip, strip), in_specs=[VMEM], out_specs=(VMEM, VMEM)
    )(velocity)
    left = lax.ppermute(hi, "space", up_col)
    right = lax.ppermute(lo, "space", down_col)
    xlo = lax.ppermute(velocity[:, count - HALO :], ROWS, up_row)
    xhi = lax.ppermute(velocity[:, :HALO], ROWS, down_row)
    corners = pl.pallas_call(
        corner_kernel, out_shape=strip, in_specs=[VMEM, VMEM], out_specs=VMEM
    )(left, right)
    below = lax.ppermute(corners, ROWS, up_row)
    above = lax.ppermute(corners, ROWS, down_row)
    wide = 2 * LANES
    nxt, filt, stress = pl.pallas_call(
        slab_kernel,
        out_shape=(
            jax.ShapeDtypeStruct(velocity.shape, F32),
            jax.ShapeDtypeStruct(velocity.shape, F32),
            jax.ShapeDtypeStruct((6,) + velocity.shape[1:], F32),
        ),
        in_specs=[VMEM] * 7,
        out_specs=(VMEM, VMEM, VMEM),
        scratch_shapes=[
            pltpu.VMEM((3, count + 2 * HALO, levels, wide), F32),
            pltpu.VMEM((3, count + 2 * HALO - 2, levels, wide), F32),
        ],
        compiler_params=params(32),
    )(velocity, xlo, xhi, left, right, below, above)

    tables = (patch_live, corner_x, corner_z, corner_y, patch_dest)
    where = jnp.stack([table_entry(t, my_row, my_col) for t in tables] + [my_row]).astype(jnp.int32)
    parts = train_call(where, filt, stress, conv_first, conv_mid, conv_last, row_count)

    shares = lax.all_to_all(parts, EVERY, 0, 0, tiled=True)
    mine = jnp.sum(shares, axis=0, keepdims=True)
    summed = lax.all_to_all(jnp.broadcast_to(mine, parts.shape), EVERY, 0, 0, tiled=True)
    grad_first, grad_mid, grad_last, loss = pl.pallas_call(
        unpack_kernel,
        out_shape=(
            jax.ShapeDtypeStruct((27, 64, 3), F32),
            jax.ShapeDtypeStruct((27, 64, 64), F32),
            jax.ShapeDtypeStruct((6, 64), F32),
            jax.ShapeDtypeStruct((1,), F32),
        ),
        in_specs=[SMEM, VMEM],
        out_specs=(VMEM, VMEM, VMEM, SMEM),
        compiler_params=params(16),
    )(where, summed)
    return (nxt, filt, stress, grad_first, grad_mid, grad_last, loss)


def solution(mesh):
    block = P(None, ("group", "dp"), None, "space")
    in_specs = (block,) + (P(),) * 8
    out_specs = (block, block, block, P(), P(), P(), P(("group", "dp")))
    return jax.shard_map(local, mesh=mesh, in_specs=in_specs, out_specs=out_specs, check_vma=False)
```

```python
import functools

import jax
import jax.numpy as jnp
from jax import lax
from jax.experimental import pallas as pl
from jax.experimental.pallas import tpu as pltpu
from jax.sharding import PartitionSpec as P

PE = 16
CELLS = PE * PE
LIVE_ROW = 2
HALO = 5
WINDOW = 32
PAIRS = [(0, 0), (1, 1), (2, 2), (0, 1), (0, 2), (1, 2)]
LANES = 128
ROWS = ("group", "dp")
EVERY = ("group", "dp", "space")
VIEWS = [(dz, dy) for dz in (-1, 0, 1) for dy in (-1, 0, 1)]
F32 = jnp.float32
BF16 = jnp.bfloat16


def lane_of(shape):
    return lax.broadcasted_iota(jnp.int32, shape, len(shape) - 1)


def roll(value, shift, axis=1):
    size = value.shape[axis]
    if isinstance(shift, int):
        shift = shift % size
        if shift == 0:
            return value
    return pltpu.roll(value, shift, axis)


def pack_kernel(vel, lo, hi):
    count = vel.shape[1]
    lane = lane_of((vel.shape[2], LANES))
    for c in range(3):
        first = jnp.zeros(lane.shape, F32)
        last = jnp.zeros(lane.shape, F32)
        for r in range(count):
            here = (lane >= HALO * r) & (lane < HALO * r + HALO)
            row = vel[c, r]
            first = jnp.where(here, roll(row, HALO * r), first)
            last = jnp.where(here, roll(row, HALO * r + HALO), last)
        lo[c] = first
        hi[c] = last


def faces(vel, left, right, up, down):
    count = vel.shape[1]
    lane = lane_of((left.shape[1], LANES))
    wide = HALO * HALO
    for c in range(3):
        lhs = left[c]
        rhs = right[c]
        up[c, 0:HALO] = vel[c, count - HALO :]
        down[c, 0:HALO] = vel[c, 0:HALO]
        at = HALO * (count - HALO)
        up[c, HALO] = jnp.where(lane < wide, roll(lhs, -at), roll(rhs, wide - at))
        down[c, HALO] = jnp.where(lane < wide, lhs, roll(rhs, wide))


def products(a, b, c):
    return [a * a, b * b, c * c, a * b, a * c, b * c]


def along_x(rows):
    return (
        20.0 * rows[3]
        + 15.0 * (rows[2] + rows[4])
        + 6.0 * (rows[1] + rows[5])
        + (rows[0] + rows[6])
    )


def solver_kernel(vel, xlo, xhi, left, right, nxt, wide_next, wa, wb):
    count = vel.shape[1]
    levels = vel.shape[2]
    lane = lane_of((levels, LANES))
    wide = HALO * HALO
    for c in range(3):
        for r in range(count + 2 * HALO):
            if r < HALO:
                main = xlo[c, r]
                lsrc, lat = xlo[c, HALO], HALO * r
                rsrc, rat = xlo[c, HALO], wide + HALO * r
            elif r < count + HALO:
                q = r - HALO
                main = vel[c, q]
                lsrc, lat = left[c], HALO * q
                rsrc, rat = right[c], HALO * q
            else:
                q = r - HALO - count
                main = xhi[c, q]
                lsrc, lat = xhi[c, HALO], HALO * q
                rsrc, rat = xhi[c, HALO], wide + HALO * q
            wa[c, r, :, 0:LANES] = main
            wa[c, r, :, LANES:] = jnp.where(
                lane < 64, roll(rsrc, -rat), roll(lsrc, LANES - HALO - lat)
            )
    level = lax.broadcasted_iota(jnp.int32, (levels, 2 * LANES), 0)

    def step(src, dst, n):
        def body(r, carry):
            mids = [src[c, r + 1] for c in range(3)]
            for c in range(3):
                mid = mids[c]
                xp = src[c, r + 2]
                xm = src[c, r]
                yp = roll(mid, -1)
                ym = roll(mid, 1)
                zp = jnp.where(level == levels - 1, 0.0, roll(mid, -1, 0))
                zm = jnp.where(level == 0, 0.0, roll(mid, 1, 0))
                adv = mids[0] * (xp - xm) + mids[1] * (yp - ym) + mids[2] * (zp - zm)
                lap = (xp + xm) + (yp + ym) + (zp + zm) - 6.0 * mid
                dst[c, r] = mid + (0.005 * lap - 0.025 * adv)
            return carry

        lax.fori_loop(0, n, body, 0)

    step(wa, wb, count + 2 * HALO - 2)
    step(wb, wide_next, count + 2 * HALO - 4)
    for c in range(3):
        nxt[c] = wide_next[c, 3 : 3 + count, :, 0:LANES]


def filter_kernel(wa, filt, stress):
    count = filt.shape[1]
    levels = filt.shape[2]
    tile = 8
    lanes = lane_of((tile, LANES))

    def along_y(f):
        m, e = f[:, :LANES], f[:, LANES:]

        def tap(k):
            outside = (lanes >= LANES - k) if k > 0 else (lanes < -k)
            return jnp.where(outside, roll(e, -k), roll(m, -k))

        near = 15.0 * (tap(1) + tap(-1)) + 6.0 * (tap(2) + tap(-2))
        return (20.0 * m + near + (tap(3) + tap(-3))) * (1.0 / 4096.0)

    def filter_row(r, carry):
        for t in range(levels // tile):
            zs = slice(t * tile, (t + 1) * tile)
            rows = [[wa[c, r + k, zs, :] for k in range(7)] for c in range(3)]
            done = [along_y(along_x(rows[c])) for c in range(3)]
            for c in range(3):
                filt[c, r, zs, :] = done[c]
            small = products(*done)
            for i, (a, b) in enumerate(PAIRS):
                big = along_y(along_x([rows[a][k] * rows[b][k] for k in range(7)]))
                stress[i, r, zs, :] = big - small[i]
        return carry

    lax.fori_loop(0, count, filter_row, 0)


def window_row(main, left, right, r, begin):
    lane = lane_of((8, LANES))
    col = (lane & (WINDOW - 1)) + (begin - HALO)
    out = jnp.zeros((8, LANES), F32)
    for t in range(4):
        zs = slice(8 * t, 8 * t + 8)
        base = 2 * LANES + WINDOW * t - begin
        a = roll(main[zs], lax.rem(base + HALO, LANES))
        b = roll(left[zs], lax.rem(base - HALO * r, LANES))
        c = roll(right[zs], lax.rem(base + LANES + HALO - HALO * r, LANES))
        value = jnp.where(col < 0, b, jnp.where(col >= LANES, c, a))
        out = jnp.where(lane // WINDOW == t, value, out)
    return out


def edge_kernel(rows, tables, vel, left, right, up, down):
    col = lax.axis_index("space")
    row = lax.axis_index("group") * lax.axis_size("dp") + lax.axis_index("dp")
    count = vel.shape[1]
    begin_up = tables[4, lax.rem(row + 1, rows), col]
    begin_down = tables[4, lax.rem(row + rows - 1, rows), col]
    for c in range(3):
        for k in range(HALO):
            r = count - HALO + k
            up[c, k] = window_row(vel[c, r], left[c], right[c], r, begin_up)
            down[c, k] = window_row(vel[c, k], left[c], right[c], k, begin_down)


def own_kernel(tables, vel, left, right, out, up, down):
    col = lax.axis_index("space")
    row = lax.axis_index("group") * lax.axis_size("dp") + lax.axis_index("dp")
    begin = tables[4, row, col]

    def body(r, carry):
        for c in range(3):
            out[c, r] = window_row(vel[c, r], left[c], right[c], r, begin)
        return carry

    lax.fori_loop(0, vel.shape[1], body, 0, unroll=4)
    faces(vel, left, right, up, down)


def window_fields(bx, own, wlo, whi, wa, wb, wc, fields):
    count = own.shape[1]
    wa[:, 0:HALO] = wlo[...]
    wa[:, HALO : HALO + count] = own[...]
    wa[:, HALO + count :] = whi[...]
    lane = lane_of((8, LANES))
    level = lax.broadcasted_iota(jnp.int32, (8, LANES), 0)

    def step(src, dst, base, n):
        for r in range(n):
            mids = [src[c, base + r + 1] for c in range(3)]
            for c in range(3):
                mid = mids[c]
                xp = src[c, base + r + 2]
                xm = src[c, base + r]
                yp = roll(mid, -1)
                ym = roll(mid, 1)
                zp = roll(mid, -1, 0)
                zp = jnp.where(
                    level == 7, jnp.where(lane >= 3 * WINDOW, 0.0, roll(zp, -WINDOW)), zp
                )
                zm = roll(mid, 1, 0)
                zm = jnp.where(level == 0, jnp.where(lane < WINDOW, 0.0, roll(zm, WINDOW)), zm)
                adv = mids[0] * (xp - xm) + mids[1] * (yp - ym) + mids[2] * (zp - zm)
                lap = (xp + xm) + (yp + ym) + (zp + zm) - 6.0 * mid
                dst[c, r] = mid + (0.005 * lap - 0.025 * adv)

    step(wa, wb, bx, PE + 8)
    step(wb, wc, 0, PE + 6)

    def along_y(f):
        near = 15.0 * (roll(f, -1) + roll(f, 1)) + 6.0 * (roll(f, -2) + roll(f, 2))
        return (20.0 * f + near + (roll(f, -3) + roll(f, 3))) * (1.0 / 4096.0)

    for r in range(PE):
        rows = [[wc[c, r + k] for k in range(7)] for c in range(3)]
        done = [along_y(along_x(rows[c])) for c in range(3)]
        at = slice(r * 8, r * 8 + 8)
        for c in range(3):
            fields[c, at] = done[c]
        small = products(*done)
        for i, (a, b) in enumerate(PAIRS):
            big = along_y(along_x([rows[a][k] * rows[b][k] for k in range(7)]))
            fields[3 + i, at] = big - small[i]


def views_of(even, odd):
    lane = lane_of(even.shape)
    column = lane & (PE - 1)
    none = jnp.zeros_like(even)
    by_y = {
        0: (even, odd),
        1: tuple(jnp.where(column == PE - 1, none, roll(h, -1)) for h in (even, odd)),
        -1: tuple(jnp.where(column == 0, none, roll(h, 1)) for h in (even, odd)),
    }
    by_z = {}
    for dy, (a, b) in by_y.items():
        by_z[0, dy] = (a, b)
        by_z[1, dy] = (b, jnp.where(lane >= LANES - PE, none, roll(a, -PE)))
        by_z[-1, dy] = (jnp.where(lane < PE, none, roll(b, PE)), a)
    return [by_z[view] for view in VIEWS]


def silu_parts(value):
    sigmoid = 0.5 * jnp.tanh(0.5 * value) + 0.5
    return value * sigmoid, sigmoid * (1.0 + value * (1.0 - sigmoid))


def dot_nn(a, b):
    return lax.dot_general(a, b, (((1,), (0,)), ((), ())), preferred_element_type=F32)


def dot_nt(a, b):
    return lax.dot_general(a, b, (((1,), (1,)), ((), ())), preferred_element_type=F32)


def cols(x, offset=0):
    return slice((x + offset) * CELLS, (x + offset + 1) * CELLS)


def half_cols(x, half):
    return slice(x * CELLS + half * LANES, x * CELLS + half * LANES + LANES)


def store_views(to, x, values, height):
    for k, pair in enumerate(views_of(values[:, :LANES], values[:, LANES:])):
        for half in range(2):
            to[height * k : height * (k + 1), half_cols(x, half)] = pair[half]


def train_kernel(
    grad_scale,
    tables,
    own,
    wlo,
    whi,
    w1,
    w2,
    w2b,
    wl,
    wlt,
    out,
    wa,
    wb,
    wc,
    fields,
    src,
    tgt,
    xv,
    vv,
    gv,
    ya,
    yb,
    s1,
    gs,
    acc,
):
    col = lax.axis_index("space")
    row = lax.axis_index("group") * lax.axis_size("dp") + lax.axis_index("dp")
    live = tables[0, row, col]

    @pl.when(live == 0)
    def _():
        out[...] = jnp.zeros(out.shape, F32)

    @pl.when(live != 0)
    def _():
        bx, bz, dest = tables[1, row, col], tables[2, row, col], tables[3, row, col]
        window_fields(bx, own, wlo, whi, wa, wb, wc, fields)
        src[...] = jnp.zeros(src.shape, F32)
        tgt[...] = jnp.zeros(tgt.shape, F32)
        lane16 = lane_of((PE, LANES)) // PE
        for f in range(9):
            halves = [jnp.zeros((PE, LANES), F32)] * 2
            for z in range(PE):
                deep = bz + z
                piece = fields[f, pl.ds(lax.rem(deep, 8), PE, stride=8), :]
                from_lane = HALO + WINDOW * (deep // 8)
                moved = roll(piece, lax.rem(PE * (z // 2) - from_lane + 2 * LANES, LANES))
                halves[z % 2] = jnp.where(lane16 == z // 2, moved, halves[z % 2])
            to, g = (src, f) if f < 3 else (tgt, f - 3)
            for half in range(2):
                to[half, PE * g : PE * g + PE] = halves[half].astype(BF16).astype(F32)

        def row_of(ref, x):
            return jnp.concatenate(
                [ref[half, pl.ds(x, 8, stride=PE), :] for half in range(2)], axis=1
            )

        for x in range(PE):
            store_views(xv, x, row_of(src, x), 8)
        xv[:, PE * CELLS :] = jnp.zeros((xv.shape[0], 2 * CELLS), F32)
        edge = jnp.zeros((192, CELLS), F32)
        ya[:, 0:CELLS] = edge
        yb[:, 0:CELLS] = edge
        yb[:, (PE + 1) * CELLS :] = edge
        none = jnp.zeros((64, CELLS), BF16)
        gs[0:64, PE * CELLS : (PE + 1) * CELLS] = none
        gs[128:192, CELLS : 2 * CELLS] = none

        def forward(yy, x):
            return yy[0:64, cols(x)] + yy[64:128, cols(x, 1)] + yy[128:192, cols(x, 2)]

        def backward(yy, x):
            return yy[0:64, cols(x, 2)] + yy[64:128, cols(x, 1)] + yy[128:192, cols(x)]

        def conv_a(x):
            ya[:, cols(x, 1)] = dot_nn(w1[...], xv[:, cols(x)].astype(BF16))

        def hidden_a(x):
            hidden, slope = silu_parts(forward(ya, x))
            s1[:, cols(x)] = slope
            store_views(vv, x, hidden.astype(BF16), 64)

        conv_a(0)
        conv_a(1)
        conv_a(2)
        hidden_a(0)

        def ahead(x):
            done = dot_nn(w2[...], vv[:, cols(x, -1)])
            conv_a(x + 2)
            hidden_a(x)
            yb[:, cols(x)] = done

        for x in range(1, PE):
            ahead(x)
        yb[:, cols(PE)] = dot_nn(w2[...], vv[:, cols(PE - 1)])

        def last(x, carry):
            total, grad_last = carry
            hidden, slope = silu_parts(forward(yb, x))
            hidden = hidden.astype(BF16)
            miss = dot_nn(wl[...], hidden) - row_of(tgt, x)
            total = total + miss * miss
            grad_pred = (miss * grad_scale).astype(BF16)
            grad_last = grad_last + dot_nt(grad_pred, hidden)
            grad = (dot_nn(wlt[...], grad_pred) * slope).astype(BF16)
            store_views(gv, x, grad, 64)
            gs[0:64, cols(x)] = grad
            gs[64:128, cols(x, 1)] = grad
            gs[128:192, cols(x, 2)] = grad
            return total, grad_last

        def back(x, carry):
            done = dot_nn(w2b[...], gv[:, cols(x, -1)])
            carry = last(x, carry)
            ya[:, cols(x)] = done
            return carry

        zero = (jnp.zeros((8, CELLS), F32), jnp.zeros((8, 64), F32))
        carry = last(0, zero)
        for x in range(1, PE):
            carry = back(x, carry)
        total, grad_last = carry
        ya[:, cols(PE)] = dot_nn(w2b[...], gv[:, cols(PE - 1)])
        ya[:, (PE + 1) * CELLS : (PE + 2) * CELLS] = edge

        acc[...] = jnp.zeros(acc.shape, F32)

        def weight_b(i):
            at = slice(2 * i * CELLS, 2 * (i + 1) * CELLS)
            at1 = slice((2 * i + 1) * CELLS, (2 * i + 3) * CELLS)
            more = dot_nt(gs[:, at1], vv[:, at])
            for k in range(2):
                x = 2 * i + k
                gv[0:64, cols(x)] = (backward(ya, x) * s1[:, cols(x)]).astype(BF16)
            acc[...] += more

        for i in range(PE // 2):
            weight_b(i)
        gs[0:64, PE * CELLS : (PE + 1) * CELLS] = none
        g1 = gv[0:64, 0 : PE * CELLS]
        shift = jnp.zeros((64, CELLS), BF16)
        whole = PE * CELLS
        stacked = jnp.concatenate(
            [
                jnp.concatenate([g1[:, CELLS:], shift], axis=1),
                g1,
                jnp.concatenate([shift, g1[:, : whole - CELLS]], axis=1),
            ],
            axis=0,
        )
        grad_first = dot_nt(xv[:, 0:whole].astype(BF16), stacked)

        for i in range(24):
            for j in range(4):
                out[4 * i + j] = acc[8 * i : 8 * i + 8, LANES * j : LANES * (j + 1)]
        for i in range(12):
            out[96 + i] = jnp.concatenate(
                [acc[8 * i : 8 * i + 8, 512:576], acc[8 * i + 96 : 8 * i + 104, 512:576]], axis=1
            )
        for i in range(9):
            out[108 + i] = grad_first[8 * i : 8 * i + 8, 0:LANES]
        for i in range(5):
            j = min(i + 5, 8)
            out[117 + i] = jnp.concatenate(
                [grad_first[8 * i : 8 * i + 8, 128:192], grad_first[8 * j : 8 * j + 8, 128:192]],
                axis=1,
            )
        loss = jnp.sum(total) * (1.0 / (PE**3 * LIVE_ROW))
        corner = lane_of((8, LANES))
        deep = lax.broadcasted_iota(jnp.int32, (8, LANES), 0)
        padded = jnp.concatenate([grad_last, jnp.zeros((8, 64), F32)], axis=1)
        out[122] = jnp.where((deep == 7) & (corner == 64 + dest), loss, padded)
        for i in range(123, 128):
            out[i] = jnp.zeros((8, LANES), F32)


def unpack_kernel(parts, first, mid, last, loss):
    for dx in range(3):
        for t in range(8):
            i = 8 * dx + t
            for k in range(9):
                if k < 8:
                    block, half = parts[4 * i + k // 2], k % 2
                else:
                    block, half = parts[96 + i % 12], i // 12
                mid[9 * dx + k, 8 * t : 8 * t + 8, :] = block[:, 64 * half : 64 * half + 64]
    for k in range(9):
        tail = parts[117 + k % 5]
        half = k // 5
        wide = jnp.concatenate([parts[108 + k], tail[:, 64 * half : 64 * half + 64]], axis=1)
        turned = wide.T
        for dx in range(3):
            first[9 * dx + k] = turned[64 * dx : 64 * dx + 64, 0:3]
    final = parts[122]
    last[...] = final[0:6, 0:64]
    corner = lane_of((8, LANES))
    deep = lax.broadcasted_iota(jnp.int32, (8, LANES), 0)
    row = lax.axis_index("group") * lax.axis_size("dp") + lax.axis_index("dp")
    mine = (deep == 7) & (corner == 64 + row)
    loss[0] = jnp.sum(jnp.where(mine, final, 0.0))


VMEM = pl.BlockSpec()
SMEM = pl.BlockSpec(memory_space=pltpu.SMEM)


def params(mib):
    return pltpu.CompilerParams(vmem_limit_bytes=mib * 1024 * 1024)


def train_call(tables, own, wlo, whi, weights, row_count):
    grad_scale = 2.0 / (PE**3 * row_count * LIVE_ROW)
    whole = PE * CELLS
    height = own.shape[1] + 2 * HALO
    return pl.pallas_call(
        functools.partial(train_kernel, grad_scale),
        out_shape=jax.ShapeDtypeStruct((128, 8, LANES), F32),
        in_specs=[SMEM] + [VMEM] * 8,
        out_specs=VMEM,
        scratch_shapes=[
            pltpu.VMEM((3, height, 8, LANES), F32),
            pltpu.VMEM((3, height, 8, LANES), F32),
            pltpu.VMEM((3, height, 8, LANES), F32),
            pltpu.VMEM((9, 8 * PE, LANES), F32),
            pltpu.VMEM((2, 8 * PE, LANES), F32),
            pltpu.VMEM((2, 8 * PE, LANES), F32),
            pltpu.VMEM((72, whole + 2 * CELLS), F32),
            pltpu.VMEM((576, whole), BF16),
            pltpu.VMEM((576, whole), BF16),
            pltpu.VMEM((192, whole + 3 * CELLS), F32),
            pltpu.VMEM((192, whole + 2 * CELLS), F32),
            pltpu.VMEM((64, whole), F32),
            pltpu.VMEM((192, whole + 2 * CELLS), BF16),
            pltpu.VMEM((192, 576), F32),
        ],
        compiler_params=params(60),
        cost_estimate=pl.CostEstimate(flops=10**7, bytes_accessed=6 * 10**7, transcendentals=0),
    )(tables, own, wlo, whi, *weights)


def weight_kernel(first, mid, last, w1, w2, w2b, wl, wlt):
    none = jnp.zeros((64, 5), F32)
    for dx in range(3):
        rows = slice(64 * dx, 64 * dx + 64)
        small = []
        for k in range(9):
            small += [first[9 * dx + k].astype(F32), none]
        w1[rows] = jnp.concatenate(small, axis=1).astype(BF16)
        blocks = [mid[9 * dx + k].astype(F32) for k in range(9)]
        w2[rows] = jnp.concatenate(blocks, axis=1).astype(BF16)
        w2b[rows] = jnp.concatenate(blocks[::-1], axis=0).T.astype(BF16)
    padded = jnp.concatenate([last[...].astype(F32), jnp.zeros((2, 64), F32)], axis=0)
    wl[...] = padded.astype(BF16)
    wlt[...] = padded.T.astype(BF16)


def layer_weights(conv_first, conv_mid, conv_last):
    shapes = ((192, 72), (192, 576), (192, 576), (8, 64), (64, 8))
    return pl.pallas_call(
        weight_kernel,
        out_shape=tuple(jax.ShapeDtypeStruct(s, BF16) for s in shapes),
        in_specs=[VMEM] * 3,
        out_specs=(VMEM,) * 5,
        compiler_params=params(60),
    )(conv_first, conv_mid, conv_last)


def local(
    velocity, conv_first, conv_mid, conv_last, corner_x, corner_z, corner_y, patch_live, patch_dest
):
    row_count = patch_live.shape[0]
    _, count, levels, _ = velocity.shape
    strip = jax.ShapeDtypeStruct((3, levels, LANES), F32)
    up_row = [(i, (i + 1) % row_count) for i in range(row_count)]
    down_row = [(j, i) for i, j in up_row]
    cols_n = lax.axis_size("space")
    up_col = [(i, (i + 1) % cols_n) for i in range(cols_n)]
    down_col = [(j, i) for i, j in up_col]

    tables = jnp.stack([patch_live, corner_x, corner_z, patch_dest, corner_y])
    lo, hi = pl.pallas_call(
        pack_kernel,
        out_shape=(strip, strip),
        in_specs=[VMEM],
        out_specs=(VMEM, VMEM),
        compiler_params=params(60),
    )(velocity)
    left = lax.ppermute(hi, "space", up_col)
    right = lax.ppermute(lo, "space", down_col)
    edge = jax.ShapeDtypeStruct((3, HALO, 8, LANES), F32)
    up, down = pl.pallas_call(
        functools.partial(edge_kernel, row_count),
        out_shape=(edge, edge),
        in_specs=[SMEM] + [VMEM] * 3,
        out_specs=(VMEM, VMEM),
        compiler_params=params(60),
    )(tables, velocity, left, right)
    wlo = lax.ppermute(up, ROWS, up_row)
    whi = lax.ppermute(down, ROWS, down_row)
    face = jax.ShapeDtypeStruct((3, HALO + 1, levels, LANES), F32)
    own, to_up, to_down = pl.pallas_call(
        own_kernel,
        out_shape=(jax.ShapeDtypeStruct((3, count, 8, LANES), F32), face, face),
        in_specs=[SMEM] + [VMEM] * 3,
        out_specs=(VMEM,) * 3,
        compiler_params=params(60),
    )(tables, velocity, left, right)
    weights = layer_weights(conv_first, conv_mid, conv_last)
    to_up, to_down, wlo, whi, weights = lax.optimization_barrier(
        (to_up, to_down, wlo, whi, weights)
    )
    xlo = lax.ppermute(to_up, ROWS, up_row)
    xhi = lax.ppermute(to_down, ROWS, down_row)
    parts = train_call(tables, own, wlo, whi, weights, row_count)

    parts, velocity, xlo, xhi = lax.optimization_barrier((parts, velocity, xlo, xhi))
    shares = lax.all_to_all(parts, EVERY, 0, 0, tiled=True)
    wide = 2 * LANES
    height = count + 2 * HALO
    nxt, wide_next = pl.pallas_call(
        solver_kernel,
        out_shape=(
            jax.ShapeDtypeStruct(velocity.shape, F32),
            jax.ShapeDtypeStruct((3, height - 4, levels, wide), F32),
        ),
        in_specs=[VMEM] * 5,
        out_specs=(VMEM, VMEM),
        scratch_shapes=[
            pltpu.VMEM((3, height, levels, wide), F32),
            pltpu.VMEM((3, height - 2, levels, wide), F32),
        ],
        compiler_params=params(60),
        cost_estimate=pl.CostEstimate(flops=10**7, bytes_accessed=4 * 10**7, transcendentals=0),
    )(velocity, xlo, xhi, left, right)
    shares, wide_next = lax.optimization_barrier((shares, wide_next))
    filt, stress = pl.pallas_call(
        filter_kernel,
        out_shape=(
            jax.ShapeDtypeStruct(velocity.shape, F32),
            jax.ShapeDtypeStruct((6,) + velocity.shape[1:], F32),
        ),
        in_specs=[VMEM],
        out_specs=(VMEM, VMEM),
        compiler_params=params(60),
        cost_estimate=pl.CostEstimate(flops=10**7, bytes_accessed=4 * 10**7, transcendentals=0),
    )(wide_next)
    mine = jnp.sum(shares, axis=0, keepdims=True)
    summed = lax.all_to_all(jnp.broadcast_to(mine, parts.shape), EVERY, 0, 0, tiled=True)
    grad_first, grad_mid, grad_last, loss = pl.pallas_call(
        unpack_kernel,
        out_shape=(
            jax.ShapeDtypeStruct((27, 64, 3), F32),
            jax.ShapeDtypeStruct((27, 64, 64), F32),
            jax.ShapeDtypeStruct((6, 64), F32),
            jax.ShapeDtypeStruct((1,), F32),
        ),
        in_specs=[VMEM],
        out_specs=(VMEM, VMEM, VMEM, SMEM),
        compiler_params=params(60),
    )(summed)
    return (nxt, filt, stress, grad_first, grad_mid, grad_last, loss)


def solution(mesh):
    block = P(None, ("group", "dp"), None, "space")
    in_specs = (block,) + (P(),) * 8
    out_specs = (block, block, block, P(), P(), P(), P(("group", "dp")))
    return jax.shard_map(local, mesh=mesh, in_specs=in_specs, out_specs=out_specs, check_vma=False)
```

```python
import functools

import jax
import jax.numpy as jnp
from jax import lax
from jax.experimental import pallas as pl
from jax.experimental.pallas import tpu as pltpu
from jax.sharding import PartitionSpec as P

PE = 16
CELLS = PE * PE
LIVE_ROW = 2
HALO = 5
WINDOW = 32
PAIRS = [(0, 0), (1, 1), (2, 2), (0, 1), (0, 2), (1, 2)]
LANES = 128
ROWS = ("group", "dp")
EVERY = ("group", "dp", "space")
VIEWS = [(dz, dy) for dz in (-1, 0, 1) for dy in (-1, 0, 1)]
F32 = jnp.float32
BF16 = jnp.bfloat16


def lane_of(shape):
    return lax.broadcasted_iota(jnp.int32, shape, len(shape) - 1)


def roll(value, shift, axis=1):
    size = value.shape[axis]
    if isinstance(shift, int):
        shift = shift % size
        if shift == 0:
            return value
    return pltpu.roll(value, shift, axis)


def pack_kernel(vel, lo, hi):
    count = vel.shape[1]
    lane = lane_of((vel.shape[2], LANES))
    for c in range(3):
        first = jnp.zeros(lane.shape, F32)
        last = jnp.zeros(lane.shape, F32)
        for r in range(count):
            here = (lane >= HALO * r) & (lane < HALO * r + HALO)
            row = vel[c, r]
            first = jnp.where(here, roll(row, HALO * r), first)
            last = jnp.where(here, roll(row, HALO * r + HALO), last)
        lo[c] = first
        hi[c] = last


def faces(vel, left, right, up, down):
    count = vel.shape[1]
    lane = lane_of((left.shape[1], LANES))
    wide = HALO * HALO
    for c in range(3):
        lhs = left[c]
        rhs = right[c]
        up[c, 0:HALO] = vel[c, count - HALO :]
        down[c, 0:HALO] = vel[c, 0:HALO]
        at = HALO * (count - HALO)
        up[c, HALO] = jnp.where(lane < wide, roll(lhs, -at), roll(rhs, wide - at))
        down[c, HALO] = jnp.where(lane < wide, lhs, roll(rhs, wide))


def products(a, b, c):
    return [a * a, b * b, c * c, a * b, a * c, b * c]


def along_x(rows):
    return (
        20.0 * rows[3]
        + 15.0 * (rows[2] + rows[4])
        + 6.0 * (rows[1] + rows[5])
        + (rows[0] + rows[6])
    )


def fetch(sources, targets, sems):
    copies = [
        pltpu.make_async_copy(source, target, sems.at[i])
        for i, (source, target) in enumerate(zip(sources, targets))
    ]
    for copy in copies:
        copy.start()
    for copy in copies:
        copy.wait()


def solver_kernel(vel, xlo_h, xhi_h, left_h, right_h, nxt, wide_next, wa, wb, xlo, xhi, left, right, sems):
    fetch((xlo_h, xhi_h, left_h, right_h), (xlo, xhi, left, right), sems)
    count = vel.shape[1]
    levels = vel.shape[2]
    lane = lane_of((levels, LANES))
    wide = HALO * HALO
    for c in range(3):
        for r in range(count + 2 * HALO):
            if r < HALO:
                main = xlo[c, r]
                lsrc, lat = xlo[c, HALO], HALO * r
                rsrc, rat = xlo[c, HALO], wide + HALO * r
            elif r < count + HALO:
                q = r - HALO
                main = vel[c, q]
                lsrc, lat = left[c], HALO * q
                rsrc, rat = right[c], HALO * q
            else:
                q = r - HALO - count
                main = xhi[c, q]
                lsrc, lat = xhi[c, HALO], HALO * q
                rsrc, rat = xhi[c, HALO], wide + HALO * q
            wa[c, r, :, 0:LANES] = main
            wa[c, r, :, LANES:] = jnp.where(
                lane < 64, roll(rsrc, -rat), roll(lsrc, LANES - HALO - lat)
            )
    level = lax.broadcasted_iota(jnp.int32, (levels, 2 * LANES), 0)

    def step(src, dst, n):
        for r in range(n):
            mids = [src[c, r + 1] for c in range(3)]
            for c in range(3):
                mid = mids[c]
                xp = src[c, r + 2]
                xm = src[c, r]
                yp = roll(mid, -1)
                ym = roll(mid, 1)
                zp = jnp.where(level == levels - 1, 0.0, roll(mid, -1, 0))
                zm = jnp.where(level == 0, 0.0, roll(mid, 1, 0))
                adv = mids[0] * (xp - xm) + mids[1] * (yp - ym) + mids[2] * (zp - zm)
                lap = (xp + xm) + (yp + ym) + (zp + zm) - 6.0 * mid
                dst[c, r] = mid + (0.005 * lap - 0.025 * adv)

    step(wa, wb, count + 2 * HALO - 2)
    step(wb, wide_next, count + 2 * HALO - 4)
    for c in range(3):
        nxt[c] = wide_next[c, 3 : 3 + count, :, 0:LANES]


def filter_kernel(wa, filt, stress, parts):
    count = filt.shape[1]
    levels = filt.shape[2]
    wide = 2 * LANES
    source = lax.broadcasted_iota(jnp.int32, (wide, LANES), 0)
    source = jnp.where(source < LANES + 64, source, source - wide)
    apart = jnp.abs(source - lax.broadcasted_iota(jnp.int32, (wide, LANES), 1))
    band = jnp.zeros((wide, LANES), F32)
    for k, weight in enumerate((20.0, 15.0, 6.0, 1.0)):
        band = jnp.where(apart == k, weight, band)
    band = jnp.concatenate([band] * 3, axis=0).astype(BF16)
    tile = 16
    for f in range(9):
        for t in range(levels // tile):
            zs = slice(t * tile, (t + 1) * tile)
            before = [None] * 6
            for r in range(count + 6):
                if f < 3:
                    value = wa[f, r, zs, :]
                else:
                    a, b = PAIRS[f - 3]
                    value = wa[a, r, zs, :] * wa[b, r, zs, :]
                for k in range(6):
                    old, before[k] = before[k], value
                    if old is None:
                        value = None
                        break
                    value = old + value
                if value is None:
                    continue
                at = slice((r - 6) * levels + t * tile, (r - 6) * levels + (t + 1) * tile)
                for k in range(3):
                    part = value.astype(BF16)
                    parts[f % 2, at, k * wide : (k + 1) * wide] = part
                    if k < 2:
                        value = value - part.astype(F32)
        done = dot_nn(parts[f % 2], band) * (1.0 / 4096.0)
        done = done.reshape(count, levels, LANES)
        if f < 3:
            filt[f] = done
        else:
            a, b = PAIRS[f - 3]
            stress[f - 3] = done - filt[a] * filt[b]


def window_row(main, left, right, r, begin):
    lane = lane_of((8, LANES))
    col = (lane & (WINDOW - 1)) + (begin - HALO)
    out = jnp.zeros((8, LANES), F32)
    for t in range(4):
        zs = slice(8 * t, 8 * t + 8)
        base = 2 * LANES + WINDOW * t - begin
        a = roll(main[zs], lax.rem(base + HALO, LANES))
        b = roll(left[zs], lax.rem(base - HALO * r, LANES))
        c = roll(right[zs], lax.rem(base + LANES + HALO - HALO * r, LANES))
        value = jnp.where(col < 0, b, jnp.where(col >= LANES, c, a))
        out = jnp.where(lane // WINDOW == t, value, out)
    return out


def edge_kernel(rows, corner_h, vel, left, right, up, down, corner_y, sems):
    col = lax.axis_index("space")
    row = lax.axis_index("group") * lax.axis_size("dp") + lax.axis_index("dp")
    fetch((corner_h,), (corner_y,), sems)
    count = vel.shape[1]
    begin_up = corner_y[col, lax.rem(row + 1, rows)]
    begin_down = corner_y[col, lax.rem(row + rows - 1, rows)]
    for c in range(3):
        for k in range(HALO):
            r = count - HALO + k
            up[c, k] = window_row(vel[c, r], left[c], right[c], r, begin_up)
            down[c, k] = window_row(vel[c, k], left[c], right[c], k, begin_down)


def own_kernel(corner_h, vel, left, right, out, up, down, corner_y, sems):
    fetch((corner_h,), (corner_y,), sems)
    col = lax.axis_index("space")
    row = lax.axis_index("group") * lax.axis_size("dp") + lax.axis_index("dp")
    begin = corner_y[col, row]

    def body(r, carry):
        for c in range(3):
            out[c, r] = window_row(vel[c, r], left[c], right[c], r, begin)
        return carry

    lax.fori_loop(0, vel.shape[1], body, 0, unroll=4)
    faces(vel, left, right, up, down)


def window_fields(bx, own, wlo, whi, wa, wb, wc, fields):
    count = own.shape[1]
    wa[:, 0:HALO] = wlo[...]
    wa[:, HALO : HALO + count] = own[...]
    wa[:, HALO + count :] = whi[...]
    lane = lane_of((8, LANES))
    level = lax.broadcasted_iota(jnp.int32, (8, LANES), 0)

    def step(src, dst, base, n):
        for r in range(n):
            mids = [src[c, base + r + 1] for c in range(3)]
            for c in range(3):
                mid = mids[c]
                xp = src[c, base + r + 2]
                xm = src[c, base + r]
                yp = roll(mid, -1)
                ym = roll(mid, 1)
                zp = roll(mid, -1, 0)
                zp = jnp.where(
                    level == 7, jnp.where(lane >= 3 * WINDOW, 0.0, roll(zp, -WINDOW)), zp
                )
                zm = roll(mid, 1, 0)
                zm = jnp.where(level == 0, jnp.where(lane < WINDOW, 0.0, roll(zm, WINDOW)), zm)
                adv = mids[0] * (xp - xm) + mids[1] * (yp - ym) + mids[2] * (zp - zm)
                lap = (xp + xm) + (yp + ym) + (zp + zm) - 6.0 * mid
                dst[c, r] = mid + (0.005 * lap - 0.025 * adv)

    step(wa, wb, bx, PE + 8)
    step(wb, wc, 0, PE + 6)

    def along_y(f):
        near = 15.0 * (roll(f, -1) + roll(f, 1)) + 6.0 * (roll(f, -2) + roll(f, 2))
        return (20.0 * f + near + (roll(f, -3) + roll(f, 3))) * (1.0 / 4096.0)

    for r in range(PE):
        rows = [[wc[c, r + k] for k in range(7)] for c in range(3)]
        done = [along_y(along_x(rows[c])) for c in range(3)]
        at = slice(r * 8, r * 8 + 8)
        for c in range(3):
            fields[c, at] = done[c]
        small = products(*done)
        for i, (a, b) in enumerate(PAIRS):
            big = along_y(along_x([rows[a][k] * rows[b][k] for k in range(7)]))
            fields[3 + i, at] = big - small[i]


def views_of(even, odd):
    lane = lane_of(even.shape)
    column = lane & (PE - 1)
    none = jnp.zeros_like(even)
    by_y = {
        0: (even, odd),
        1: tuple(jnp.where(column == PE - 1, none, roll(h, -1)) for h in (even, odd)),
        -1: tuple(jnp.where(column == 0, none, roll(h, 1)) for h in (even, odd)),
    }
    by_z = {}
    for dy, (a, b) in by_y.items():
        by_z[0, dy] = (a, b)
        by_z[1, dy] = (b, jnp.where(lane >= LANES - PE, none, roll(a, -PE)))
        by_z[-1, dy] = (jnp.where(lane < PE, none, roll(b, PE)), a)
    return [by_z[view] for view in VIEWS]


def silu_parts(value):
    sigmoid = 0.5 * jnp.tanh(0.5 * value) + 0.5
    return value * sigmoid, sigmoid * (1.0 + value * (1.0 - sigmoid))


def dot_nn(a, b):
    return lax.dot_general(a, b, (((1,), (0,)), ((), ())), preferred_element_type=F32)


def dot_nt(a, b):
    return lax.dot_general(a, b, (((1,), (1,)), ((), ())), preferred_element_type=F32)


def cols(x, offset=0):
    return slice((x + offset) * CELLS, (x + offset + 1) * CELLS)


def half_cols(x, half):
    return slice(x * CELLS + half * LANES, x * CELLS + half * LANES + LANES)


def store_views(to, x, values, height):
    for k, pair in enumerate(views_of(values[:, :LANES], values[:, LANES:])):
        for half in range(2):
            to[height * k : height * (k + 1), half_cols(x, half)] = pair[half]


def train_kernel(
    grad_scale,
    patch_live,
    corner_x,
    corner_z,
    patch_dest,
    own,
    wlo,
    whi,
    w1,
    w2,
    w2b,
    wl,
    wlt,
    out,
    wa,
    wb,
    wc,
    fields,
    src,
    tgt,
    xv,
    vv,
    gv,
    ya,
    yb,
    s1,
    gs,
    acc,
):
    col = lax.axis_index("space")
    row = lax.axis_index("group") * lax.axis_size("dp") + lax.axis_index("dp")
    live = patch_live[col, row]

    @pl.when(live == 0)
    def _():
        out[...] = jnp.zeros(out.shape, F32)

    @pl.when(live != 0)
    def _():
        bx, bz, dest = corner_x[col, row], corner_z[col, row], patch_dest[col, row]
        window_fields(bx, own, wlo, whi, wa, wb, wc, fields)
        src[...] = jnp.zeros(src.shape, F32)
        tgt[...] = jnp.zeros(tgt.shape, F32)
        lane16 = lane_of((PE, LANES)) // PE
        for f in range(9):
            halves = [jnp.zeros((PE, LANES), F32)] * 2
            for z in range(PE):
                deep = bz + z
                piece = fields[f, pl.ds(lax.rem(deep, 8), PE, stride=8), :]
                from_lane = HALO + WINDOW * (deep // 8)
                moved = roll(piece, lax.rem(PE * (z // 2) - from_lane + 2 * LANES, LANES))
                halves[z % 2] = jnp.where(lane16 == z // 2, moved, halves[z % 2])
            to, g = (src, f) if f < 3 else (tgt, f - 3)
            for half in range(2):
                to[half, PE * g : PE * g + PE] = halves[half].astype(BF16).astype(F32)

        def row_of(ref, x):
            return jnp.concatenate(
                [ref[half, pl.ds(x, 8, stride=PE), :] for half in range(2)], axis=1
            )

        for x in range(PE):
            store_views(xv, x, row_of(src, x), 8)
        xv[:, PE * CELLS :] = jnp.zeros((xv.shape[0], 2 * CELLS), F32)
        edge = jnp.zeros((192, CELLS), F32)
        ya[:, 0:CELLS] = edge
        yb[:, 0:CELLS] = edge
        yb[:, (PE + 1) * CELLS :] = edge
        none = jnp.zeros((64, CELLS), BF16)
        gs[0:64, PE * CELLS : (PE + 1) * CELLS] = none
        gs[128:192, CELLS : 2 * CELLS] = none

        def forward(yy, x):
            return yy[0:64, cols(x)] + yy[64:128, cols(x, 1)] + yy[128:192, cols(x, 2)]

        def backward(yy, x):
            return yy[0:64, cols(x, 2)] + yy[64:128, cols(x, 1)] + yy[128:192, cols(x)]

        def conv_a(x):
            ya[:, cols(x, 1)] = dot_nn(w1[...], xv[:, cols(x)].astype(BF16))

        def hidden_a(x):
            hidden, slope = silu_parts(forward(ya, x))
            s1[:, cols(x)] = slope
            store_views(vv, x, hidden.astype(BF16), 64)

        conv_a(0)
        conv_a(1)
        conv_a(2)
        hidden_a(0)

        def ahead(x):
            done = dot_nn(w2[...], vv[:, cols(x, -1)])
            conv_a(x + 2)
            hidden_a(x)
            yb[:, cols(x)] = done

        for x in range(1, PE):
            ahead(x)
        yb[:, cols(PE)] = dot_nn(w2[...], vv[:, cols(PE - 1)])

        def last(x, carry):
            total, grad_last = carry
            hidden, slope = silu_parts(forward(yb, x))
            hidden = hidden.astype(BF16)
            miss = dot_nn(wl[...], hidden) - row_of(tgt, x)
            total = total + miss * miss
            grad_pred = (miss * grad_scale).astype(BF16)
            grad_last = grad_last + dot_nt(grad_pred, hidden)
            grad = (dot_nn(wlt[...], grad_pred) * slope).astype(BF16)
            store_views(gv, x, grad, 64)
            gs[0:64, cols(x)] = grad
            gs[64:128, cols(x, 1)] = grad
            gs[128:192, cols(x, 2)] = grad
            return total, grad_last

        def back(x, carry):
            done = dot_nn(w2b[...], gv[:, cols(x, -1)])
            carry = last(x, carry)
            ya[:, cols(x)] = done
            return carry

        zero = (jnp.zeros((8, CELLS), F32), jnp.zeros((8, 64), F32))
        carry = last(0, zero)
        for x in range(1, PE):
            carry = back(x, carry)
        total, grad_last = carry
        ya[:, cols(PE)] = dot_nn(w2b[...], gv[:, cols(PE - 1)])
        ya[:, (PE + 1) * CELLS : (PE + 2) * CELLS] = edge

        acc[...] = jnp.zeros(acc.shape, F32)

        def weight_b(i):
            at = slice(2 * i * CELLS, 2 * (i + 1) * CELLS)
            at1 = slice((2 * i + 1) * CELLS, (2 * i + 3) * CELLS)
            more = dot_nt(gs[:, at1], vv[:, at])
            for k in range(2):
                x = 2 * i + k
                gv[0:64, cols(x)] = (backward(ya, x) * s1[:, cols(x)]).astype(BF16)
            acc[...] += more

        for i in range(PE // 2):
            weight_b(i)
        gs[0:64, PE * CELLS : (PE + 1) * CELLS] = none
        g1 = gv[0:64, 0 : PE * CELLS]
        shift = jnp.zeros((64, CELLS), BF16)
        whole = PE * CELLS
        stacked = jnp.concatenate(
            [
                jnp.concatenate([g1[:, CELLS:], shift], axis=1),
                g1,
                jnp.concatenate([shift, g1[:, : whole - CELLS]], axis=1),
            ],
            axis=0,
        )
        grad_first = dot_nt(xv[:, 0:whole].astype(BF16), stacked)

        for i in range(24):
            for j in range(4):
                out[4 * i + j] = acc[8 * i : 8 * i + 8, LANES * j : LANES * (j + 1)]
        for i in range(12):
            out[96 + i] = jnp.concatenate(
                [acc[8 * i : 8 * i + 8, 512:576], acc[8 * i + 96 : 8 * i + 104, 512:576]], axis=1
            )
        for i in range(9):
            out[108 + i] = grad_first[8 * i : 8 * i + 8, 0:LANES]
        for i in range(5):
            j = min(i + 5, 8)
            out[117 + i] = jnp.concatenate(
                [grad_first[8 * i : 8 * i + 8, 128:192], grad_first[8 * j : 8 * j + 8, 128:192]],
                axis=1,
            )
        loss = jnp.sum(total) * (1.0 / (PE**3 * LIVE_ROW))
        corner = lane_of((8, LANES))
        deep = lax.broadcasted_iota(jnp.int32, (8, LANES), 0)
        padded = jnp.concatenate([grad_last, jnp.zeros((8, 64), F32)], axis=1)
        out[122] = jnp.where((deep == 7) & (corner == 64 + dest), loss, padded)
        for i in range(123, 128):
            out[i] = jnp.zeros((8, LANES), F32)


def unpack_kernel(parts, first, mid, last, loss):
    for dx in range(3):
        for t in range(8):
            i = 8 * dx + t
            for k in range(9):
                if k < 8:
                    block, half = parts[4 * i + k // 2], k % 2
                else:
                    block, half = parts[96 + i % 12], i // 12
                mid[9 * dx + k, 8 * t : 8 * t + 8, :] = block[:, 64 * half : 64 * half + 64]
    for k in range(9):
        tail = parts[117 + k % 5]
        half = k // 5
        head = parts[108 + k]
        by_dx = (head[:, 0:64], head[:, 64:128], tail[:, 64 * half : 64 * half + 64])
        for dx in range(3):
            for c in range(3):
                first[c, 9 * dx + k : 9 * dx + k + 1, :] = by_dx[dx][c : c + 1]
    final = parts[122]
    last[...] = final[0:6, 0:64]
    corner = lane_of((8, LANES))
    deep = lax.broadcasted_iota(jnp.int32, (8, LANES), 0)
    row = lax.axis_index("group") * lax.axis_size("dp") + lax.axis_index("dp")
    mine = (deep == 7) & (corner == 64 + row)
    loss[0] = jnp.sum(jnp.where(mine, final, 0.0))


VMEM = pl.BlockSpec()
HERE = pl.BlockSpec(memory_space=pltpu.VMEM)
AWAY = pl.BlockSpec(memory_space=pltpu.HBM)
SMEM = pl.BlockSpec(memory_space=pltpu.SMEM)


def params(mib):
    return pltpu.CompilerParams(vmem_limit_bytes=mib * 1024 * 1024)


def train_call(tables, own, wlo, whi, weights, row_count):
    grad_scale = 2.0 / (PE**3 * row_count * LIVE_ROW)
    whole = PE * CELLS
    height = own.shape[1] + 2 * HALO
    return pl.pallas_call(
        functools.partial(train_kernel, grad_scale),
        out_shape=jax.ShapeDtypeStruct((128, 8, LANES), F32),
        in_specs=[SMEM] * 4 + [HERE] * 3 + [VMEM] * 5,
        out_specs=HERE,
        scratch_shapes=[
            pltpu.VMEM((3, height, 8, LANES), F32),
            pltpu.VMEM((3, height, 8, LANES), F32),
            pltpu.VMEM((3, height, 8, LANES), F32),
            pltpu.VMEM((9, 8 * PE, LANES), F32),
            pltpu.VMEM((2, 8 * PE, LANES), F32),
            pltpu.VMEM((2, 8 * PE, LANES), F32),
            pltpu.VMEM((72, whole + 2 * CELLS), F32),
            pltpu.VMEM((576, whole), BF16),
            pltpu.VMEM((576, whole), BF16),
            pltpu.VMEM((192, whole + 3 * CELLS), F32),
            pltpu.VMEM((192, whole + 2 * CELLS), F32),
            pltpu.VMEM((64, whole), F32),
            pltpu.VMEM((192, whole + 2 * CELLS), BF16),
            pltpu.VMEM((192, 576), F32),
        ],
        compiler_params=params(40),
        cost_estimate=pl.CostEstimate(flops=10**7, bytes_accessed=6 * 10**7, transcendentals=0),
    )(*tables, own, wlo, whi, *weights)


def weight_kernel(first_h, mid_h, last_h, w1, w2, w2b, wl, wlt, small, first, mid, last, sems):
    fetch((first_h, mid_h, last_h), (first, mid, last), sems)
    small[...] = jnp.zeros(small.shape, F32)
    for c in range(3):
        value = first[c].astype(F32)
        for dx in range(3):
            small[dx, pl.ds(c, 9, stride=8), :] = value[9 * dx : 9 * dx + 9]
    for dx in range(3):
        rows = slice(64 * dx, 64 * dx + 64)
        w1[rows] = small[dx].T.astype(BF16)
        blocks = [mid[9 * dx + k].astype(F32) for k in range(9)]
        w2[rows] = jnp.concatenate(blocks, axis=1).astype(BF16)
        w2b[rows] = jnp.concatenate(blocks[::-1], axis=0).T.astype(BF16)
    padded = jnp.concatenate([last[...].astype(F32), jnp.zeros((2, 64), F32)], axis=0)
    wl[...] = padded.astype(BF16)
    wlt[...] = padded.T.astype(BF16)


def layer_weights(conv_first, conv_mid, conv_last):
    shapes = ((192, 72), (192, 576), (192, 576), (8, 64), (64, 8))
    return pl.pallas_call(
        weight_kernel,
        out_shape=tuple(jax.ShapeDtypeStruct(s, BF16) for s in shapes),
        in_specs=[AWAY] * 3,
        out_specs=(HERE,) * 5,
        scratch_shapes=[
            pltpu.VMEM((3, 72, 64), F32),
            pltpu.VMEM((3, 27, 64), BF16),
            pltpu.VMEM((27, 64, 64), BF16),
            pltpu.VMEM((6, 64), BF16),
            pltpu.SemaphoreType.DMA((3,)),
        ],
        compiler_params=params(8),
    )(conv_first.transpose(2, 0, 1), conv_mid, conv_last)


def local(
    velocity, conv_first, conv_mid, conv_last, corner_x, corner_z, corner_y, patch_live, patch_dest
):
    row_count = patch_live.shape[0]
    _, count, levels, _ = velocity.shape
    strip = jax.ShapeDtypeStruct((3, levels, LANES), F32)
    up_row = [(i, (i + 1) % row_count) for i in range(row_count)]
    down_row = [(j, i) for i, j in up_row]
    cols_n = lax.axis_size("space")
    up_col = [(i, (i + 1) % cols_n) for i in range(cols_n)]
    down_col = [(j, i) for i, j in up_col]

    tables = (patch_live.T, corner_x.T, corner_z.T, patch_dest.T)
    corner_y = corner_y.T
    corner_scratch = [pltpu.SMEM(corner_y.shape, jnp.int32), pltpu.SemaphoreType.DMA((1,))]
    lo, hi = pl.pallas_call(
        pack_kernel,
        out_shape=(strip, strip),
        in_specs=[VMEM],
        out_specs=(HERE, HERE),
        compiler_params=params(8),
    )(velocity)
    left = lax.ppermute(hi, "space", up_col)
    right = lax.ppermute(lo, "space", down_col)
    edge = jax.ShapeDtypeStruct((3, HALO, 8, LANES), F32)
    up, down = pl.pallas_call(
        functools.partial(edge_kernel, row_count),
        out_shape=(edge, edge),
        in_specs=[AWAY, VMEM, HERE, HERE],
        out_specs=(HERE, HERE),
        scratch_shapes=corner_scratch,
        compiler_params=params(8),
    )(corner_y, velocity, left, right)
    wlo = lax.ppermute(up, ROWS, up_row)
    whi = lax.ppermute(down, ROWS, down_row)
    face = jax.ShapeDtypeStruct((3, HALO + 1, levels, LANES), F32)
    own, to_up, to_down = pl.pallas_call(
        own_kernel,
        out_shape=(jax.ShapeDtypeStruct((3, count, 8, LANES), F32), face, face),
        in_specs=[AWAY, VMEM, HERE, HERE],
        out_specs=(HERE,) * 3,
        scratch_shapes=corner_scratch,
        compiler_params=params(12),
    )(corner_y, velocity, left, right)
    weights = layer_weights(conv_first, conv_mid, conv_last)
    to_up, to_down, wlo, whi, weights = lax.optimization_barrier(
        (to_up, to_down, wlo, whi, weights)
    )
    xlo = lax.ppermute(to_up, ROWS, up_row)
    xhi = lax.ppermute(to_down, ROWS, down_row)
    parts = train_call(tables, own, wlo, whi, weights, row_count)

    parts, velocity, xlo, xhi = lax.optimization_barrier((parts, velocity, xlo, xhi))
    shares = lax.all_to_all(parts, EVERY, 0, 0, tiled=True)
    wide = 2 * LANES
    height = count + 2 * HALO
    nxt, wide_next = pl.pallas_call(
        solver_kernel,
        out_shape=(
            jax.ShapeDtypeStruct(velocity.shape, F32),
            jax.ShapeDtypeStruct((3, height - 4, levels, wide), F32),
        ),
        in_specs=[VMEM] + [AWAY] * 4,
        out_specs=(VMEM, VMEM),
        scratch_shapes=[
            pltpu.VMEM((3, height, levels, wide), F32),
            pltpu.VMEM((3, height - 2, levels, wide), F32),
            pltpu.VMEM(xlo.shape, F32),
            pltpu.VMEM(xhi.shape, F32),
            pltpu.VMEM(left.shape, F32),
            pltpu.VMEM(right.shape, F32),
            pltpu.SemaphoreType.DMA((4,)),
        ],
        compiler_params=params(24),
        cost_estimate=pl.CostEstimate(flops=10**7, bytes_accessed=4 * 10**7, transcendentals=0),
    )(velocity, xlo, xhi, left, right)
    shares, wide_next = lax.optimization_barrier((shares, wide_next))
    filt, stress = pl.pallas_call(
        filter_kernel,
        out_shape=(
            jax.ShapeDtypeStruct(velocity.shape, F32),
            jax.ShapeDtypeStruct((6,) + velocity.shape[1:], F32),
        ),
        in_specs=[VMEM],
        out_specs=(VMEM, VMEM),
        scratch_shapes=[pltpu.VMEM((2, count * levels, 6 * LANES), BF16)],
        compiler_params=params(24),
        cost_estimate=pl.CostEstimate(flops=10**7, bytes_accessed=4 * 10**7, transcendentals=0),
    )(wide_next)
    mine = jnp.sum(shares, axis=0, keepdims=True)
    summed = lax.all_to_all(jnp.broadcast_to(mine, parts.shape), EVERY, 0, 0, tiled=True)
    grad_first, grad_mid, grad_last, loss = pl.pallas_call(
        unpack_kernel,
        out_shape=(
            jax.ShapeDtypeStruct((3, 27, 64), F32),
            jax.ShapeDtypeStruct((27, 64, 64), F32),
            jax.ShapeDtypeStruct((6, 64), F32),
            jax.ShapeDtypeStruct((1,), F32),
        ),
        in_specs=[HERE],
        out_specs=(VMEM, VMEM, VMEM, SMEM),
        compiler_params=params(8),
    )(summed)
    return (nxt, filt, stress, grad_first.transpose(1, 2, 0), grad_mid, grad_last, loss)


def solution(mesh):
    block = P(None, ("group", "dp"), None, "space")
    in_specs = (block,) + (P(),) * 8
    out_specs = (block, block, block, P(), P(), P(), P(("group", "dp")))
    return jax.shard_map(local, mesh=mesh, in_specs=in_specs, out_specs=out_specs, check_vma=False)
```

```python
import functools

import jax
import jax.numpy as jnp
from jax import lax
from jax.experimental import pallas as pl
from jax.experimental.pallas import tpu as pltpu
from jax.sharding import PartitionSpec as P

PE = 16
CELLS = PE * PE
LIVE_ROW = 2
HALO = 5
WINDOW = 32
PAIRS = [(0, 0), (1, 1), (2, 2), (0, 1), (0, 2), (1, 2)]
LANES = 128
ROWS = ("group", "dp")
EVERY = ("group", "dp", "space")
VIEWS = [(dz, dy) for dz in (-1, 0, 1) for dy in (-1, 0, 1)]
F32 = jnp.float32
BF16 = jnp.bfloat16


def lane_of(shape):
    return lax.broadcasted_iota(jnp.int32, shape, len(shape) - 1)


def roll(value, shift, axis=1):
    size = value.shape[axis]
    if isinstance(shift, int):
        shift = shift % size
        if shift == 0:
            return value
    return pltpu.roll(value, shift, axis)


def pack_kernel(vel, lo, hi, low_rows, high_rows):
    count = vel.shape[1]
    lane = lane_of((vel.shape[2], LANES))
    for c in range(3):
        first = jnp.zeros(lane.shape, F32)
        last = jnp.zeros(lane.shape, F32)
        for r in range(count):
            here = (lane >= HALO * r) & (lane < HALO * r + HALO)
            row = vel[c, r]
            first = jnp.where(here, roll(row, HALO * r), first)
            last = jnp.where(here, roll(row, HALO * r + HALO), last)
        lo[c] = first
        hi[c] = last
        low_rows[c] = vel[c, 0:HALO]
        high_rows[c] = vel[c, count - HALO :]


def faces(vel, left, right, up, down):
    count = vel.shape[1]
    lane = lane_of((left.shape[1], LANES))
    wide = HALO * HALO
    for c in range(3):
        lhs = left[c]
        rhs = right[c]
        up[c, 0:HALO] = vel[c, count - HALO :]
        down[c, 0:HALO] = vel[c, 0:HALO]
        at = HALO * (count - HALO)
        up[c, HALO] = jnp.where(lane < wide, roll(lhs, -at), roll(rhs, wide - at))
        down[c, HALO] = jnp.where(lane < wide, lhs, roll(rhs, wide))


def products(a, b, c):
    return [a * a, b * b, c * c, a * b, a * c, b * c]


def along_x(rows):
    return (
        20.0 * rows[3]
        + 15.0 * (rows[2] + rows[4])
        + 6.0 * (rows[1] + rows[5])
        + (rows[0] + rows[6])
    )


def fetch(sources, targets, sems):
    copies = [
        pltpu.make_async_copy(source, target, sems.at[i])
        for i, (source, target) in enumerate(zip(sources, targets))
    ]
    for copy in copies:
        copy.start()
    for copy in copies:
        copy.wait()


def solver_kernel(vel, xlo_h, xhi_h, left_h, right_h, nxt, wide_next, wa, wb, xlo, xhi, left, right, sems):
    fetch((xlo_h, xhi_h, left_h, right_h), (xlo, xhi, left, right), sems)
    count = vel.shape[1]
    levels = vel.shape[2]
    lane = lane_of((levels, LANES))
    wide = HALO * HALO
    for c in range(3):
        for r in range(count + 2 * HALO):
            if r < HALO:
                main = xlo[c, r]
                lsrc, lat = xlo[c, HALO], HALO * r
                rsrc, rat = xlo[c, HALO], wide + HALO * r
            elif r < count + HALO:
                q = r - HALO
                main = vel[c, q]
                lsrc, lat = left[c], HALO * q
                rsrc, rat = right[c], HALO * q
            else:
                q = r - HALO - count
                main = xhi[c, q]
                lsrc, lat = xhi[c, HALO], HALO * q
                rsrc, rat = xhi[c, HALO], wide + HALO * q
            wa[c, r, :, 0:LANES] = main
            wa[c, r, :, LANES:] = jnp.where(
                lane < 64, roll(rsrc, -rat), roll(lsrc, LANES - HALO - lat)
            )
    level = lax.broadcasted_iota(jnp.int32, (levels, 2 * LANES), 0)

    def step(src, dst, n):
        for r in range(n):
            mids = [src[c, r + 1] for c in range(3)]
            for c in range(3):
                mid = mids[c]
                xp = src[c, r + 2]
                xm = src[c, r]
                yp = roll(mid, -1)
                ym = roll(mid, 1)
                zp = jnp.where(level == levels - 1, 0.0, roll(mid, -1, 0))
                zm = jnp.where(level == 0, 0.0, roll(mid, 1, 0))
                adv = mids[0] * (xp - xm) + mids[1] * (yp - ym) + mids[2] * (zp - zm)
                lap = (xp + xm) + (yp + ym) + (zp + zm) - 6.0 * mid
                dst[c, r] = mid + (0.005 * lap - 0.025 * adv)

    step(wa, wb, count + 2 * HALO - 2)
    step(wb, wide_next, count + 2 * HALO - 4)
    for c in range(3):
        nxt[c] = wide_next[c, 3 : 3 + count, :, 0:LANES]


def filter_kernel(wa, filt, stress, parts):
    count = filt.shape[1]
    levels = filt.shape[2]
    wide = 2 * LANES
    source = lax.broadcasted_iota(jnp.int32, (wide, LANES), 0)
    source = jnp.where(source < LANES + 64, source, source - wide)
    apart = jnp.abs(source - lax.broadcasted_iota(jnp.int32, (wide, LANES), 1))
    band = jnp.zeros((wide, LANES), F32)
    for k, weight in enumerate((20.0, 15.0, 6.0, 1.0)):
        band = jnp.where(apart == k, weight, band)
    band = jnp.concatenate([band] * 3, axis=0).astype(BF16)
    tile = 16
    for f in range(9):
        for t in range(levels // tile):
            zs = slice(t * tile, (t + 1) * tile)
            before = [None] * 6
            for r in range(count + 6):
                if f < 3:
                    value = wa[f, r, zs, :]
                else:
                    a, b = PAIRS[f - 3]
                    value = wa[a, r, zs, :] * wa[b, r, zs, :]
                for k in range(6):
                    old, before[k] = before[k], value
                    if old is None:
                        value = None
                        break
                    value = old + value
                if value is None:
                    continue
                at = slice((r - 6) * levels + t * tile, (r - 6) * levels + (t + 1) * tile)
                for k in range(3):
                    part = value.astype(BF16)
                    parts[f % 2, at, k * wide : (k + 1) * wide] = part
                    if k < 2:
                        value = value - part.astype(F32)
        done = dot_nn(parts[f % 2], band) * (1.0 / 4096.0)
        done = done.reshape(count, levels, LANES)
        if f < 3:
            filt[f] = done
        else:
            a, b = PAIRS[f - 3]
            stress[f - 3] = done - filt[a] * filt[b]


def window_row(main, left, right, r, begin):
    lane = lane_of((8, LANES))
    col = (lane & (WINDOW - 1)) + (begin - HALO)
    out = jnp.zeros((8, LANES), F32)
    for t in range(4):
        zs = slice(8 * t, 8 * t + 8)
        base = 2 * LANES + WINDOW * t - begin
        a = roll(main[zs], lax.rem(base + HALO, LANES))
        b = roll(left[zs], lax.rem(base - HALO * r, LANES))
        c = roll(right[zs], lax.rem(base + LANES + HALO - HALO * r, LANES))
        value = jnp.where(col < 0, b, jnp.where(col >= LANES, c, a))
        out = jnp.where(lane // WINDOW == t, value, out)
    return out


def entries(word):
    return word & 1, (word >> 1) & 7, (word >> 4) & 63, (word >> 10) & 255, word >> 18


def edge_kernel(rows, count, table, low_rows, high_rows, left, right, up, down):
    col = lax.axis_index("space")
    row = lax.axis_index("group") * lax.axis_size("dp") + lax.axis_index("dp")
    begin_up = entries(table[col, lax.rem(row + 1, rows)])[3]
    begin_down = entries(table[col, lax.rem(row + rows - 1, rows)])[3]
    for c in range(3):
        for k in range(HALO):
            r = count - HALO + k
            up[c, k] = window_row(high_rows[c, k], left[c], right[c], r, begin_up)
            down[c, k] = window_row(low_rows[c, k], left[c], right[c], k, begin_down)


def own_kernel(table, vel, left, right, out, up, down):
    col = lax.axis_index("space")
    row = lax.axis_index("group") * lax.axis_size("dp") + lax.axis_index("dp")
    begin = entries(table[col, row])[3]

    def body(r, carry):
        for c in range(3):
            out[c, r] = window_row(vel[c, r], left[c], right[c], r, begin)
        return carry

    lax.fori_loop(0, vel.shape[1], body, 0, unroll=4)
    faces(vel, left, right, up, down)


def window_steps(bx, own, wlo, whi, wa, wb, wc):
    count = own.shape[1]
    wa[:, 0:HALO] = wlo[...]
    wa[:, HALO : HALO + count] = own[...]
    wa[:, HALO + count :] = whi[...]
    lane = lane_of((8, LANES))
    level = lax.broadcasted_iota(jnp.int32, (8, LANES), 0)

    def step(src, dst, base, n):
        for r in range(n):
            mids = [src[c, base + r + 1] for c in range(3)]
            for c in range(3):
                mid = mids[c]
                xp = src[c, base + r + 2]
                xm = src[c, base + r]
                yp = roll(mid, -1)
                ym = roll(mid, 1)
                zp = roll(mid, -1, 0)
                zp = jnp.where(
                    level == 7, jnp.where(lane >= 3 * WINDOW, 0.0, roll(zp, -WINDOW)), zp
                )
                zm = roll(mid, 1, 0)
                zm = jnp.where(level == 0, jnp.where(lane < WINDOW, 0.0, roll(zm, WINDOW)), zm)
                adv = mids[0] * (xp - xm) + mids[1] * (yp - ym) + mids[2] * (zp - zm)
                lap = (xp + xm) + (yp + ym) + (zp + zm) - 6.0 * mid
                dst[c, r] = mid + (0.005 * lap - 0.025 * adv)

    step(wa, wb, bx, PE + 8)
    step(wb, wc, 0, PE + 6)

    def along_y(f):
        near = 15.0 * (roll(f, -1) + roll(f, 1)) + 6.0 * (roll(f, -2) + roll(f, 2))
        return (20.0 * f + near + (roll(f, -3) + roll(f, 3))) * (1.0 / 4096.0)

    return along_y


def window_field(f, along_y, wc, fields):
    for r in range(PE):
        at = slice(r * 8, r * 8 + 8)
        if f < 3:
            fields[f, at] = along_y(along_x([wc[f, r + k] for k in range(7)]))
        else:
            a, b = PAIRS[f - 3]
            big = along_y(along_x([wc[a, r + k] * wc[b, r + k] for k in range(7)]))
            fields[f, at] = big - fields[a, at] * fields[b, at]


def views_of(even, odd):
    lane = lane_of(even.shape)
    column = lane & (PE - 1)
    none = jnp.zeros_like(even)
    by_y = {
        0: (even, odd),
        1: tuple(jnp.where(column == PE - 1, none, roll(h, -1)) for h in (even, odd)),
        -1: tuple(jnp.where(column == 0, none, roll(h, 1)) for h in (even, odd)),
    }
    by_z = {}
    for dy, (a, b) in by_y.items():
        by_z[0, dy] = (a, b)
        by_z[1, dy] = (b, jnp.where(lane >= LANES - PE, none, roll(a, -PE)))
        by_z[-1, dy] = (jnp.where(lane < PE, none, roll(b, PE)), a)
    return [by_z[view] for view in VIEWS]


def silu_parts(value):
    sigmoid = 0.5 * jnp.tanh(0.5 * value) + 0.5
    return value * sigmoid, sigmoid * (1.0 + value * (1.0 - sigmoid))


def dot_nn(a, b):
    return lax.dot_general(a, b, (((1,), (0,)), ((), ())), preferred_element_type=F32)


def dot_nt(a, b):
    return lax.dot_general(a, b, (((1,), (1,)), ((), ())), preferred_element_type=F32)


def cols(x, offset=0):
    return slice((x + offset) * CELLS, (x + offset + 1) * CELLS)


def half_cols(x, half):
    return slice(x * CELLS + half * LANES, x * CELLS + half * LANES + LANES)


def store_views(to, x, values, height):
    for k, pair in enumerate(views_of(values[:, :LANES], values[:, LANES:])):
        for half in range(2):
            to[height * k : height * (k + 1), half_cols(x, half)] = pair[half]


def layer_weights(first, mid, last, w1, w2, wl, wlt, small):
    small[...] = jnp.zeros(small.shape, F32)
    for c in range(3):
        value = first[c].astype(F32)
        for dx in range(3):
            small[dx, pl.ds(c, 9, stride=8), :] = value[9 * dx : 9 * dx + 9]
    for dx in range(3):
        rows = slice(64 * dx, 64 * dx + 64)
        w1[rows] = small[dx].T.astype(BF16)
        blocks = [mid[9 * dx + k].astype(F32) for k in range(9)]
        w2[rows] = jnp.concatenate(blocks, axis=1).astype(BF16)
    padded = jnp.concatenate([last[...].astype(F32), jnp.zeros((2, 64), F32)], axis=0)
    wl[...] = padded.astype(BF16)
    wlt[...] = padded.T.astype(BF16)


def backward_weights(dx, mid, w2b):
    blocks = [mid[9 * dx + k].astype(F32) for k in range(9)]
    w2b[64 * dx : 64 * dx + 64] = jnp.concatenate(blocks[::-1], axis=0).T.astype(BF16)


def train_kernel(
    grad_scale,
    table,
    own,
    wlo,
    whi,
    first,
    mid,
    last_w,
    out,
    w1,
    w2,
    w2b,
    wl,
    wlt,
    small,
    wa,
    wb,
    wc,
    fields,
    src,
    tgt,
    xv,
    vv,
    gv,
    ya,
    yb,
    s1,
    gs,
    acc,
):
    col = lax.axis_index("space")
    row = lax.axis_index("group") * lax.axis_size("dp") + lax.axis_index("dp")
    live, bx, bz, _, dest = entries(table[col, row])

    @pl.when(live == 0)
    def _():
        out[...] = jnp.zeros(out.shape, F32)

    @pl.when(live != 0)
    def _():
        layer_weights(first, mid, last_w, w1, w2, wl, wlt, small)
        along_y = window_steps(bx, own, wlo, whi, wa, wb, wc)
        src[...] = jnp.zeros(src.shape, F32)
        tgt[...] = jnp.zeros(tgt.shape, F32)
        lane16 = lane_of((PE, LANES)) // PE

        def extract(f):
            window_field(f, along_y, wc, fields)
            halves = [jnp.zeros((PE, LANES), F32)] * 2
            for z in range(PE):
                deep = bz + z
                piece = fields[f, pl.ds(lax.rem(deep, 8), PE, stride=8), :]
                from_lane = HALO + WINDOW * (deep // 8)
                moved = roll(piece, lax.rem(PE * (z // 2) - from_lane + 2 * LANES, LANES))
                halves[z % 2] = jnp.where(lane16 == z // 2, moved, halves[z % 2])
            to, g = (src, f) if f < 3 else (tgt, f - 3)
            for half in range(2):
                to[half, PE * g : PE * g + PE] = halves[half].astype(BF16).astype(F32)

        for f in range(3):
            extract(f)

        def row_of(ref, x):
            return jnp.concatenate(
                [ref[half, pl.ds(x, 8, stride=PE), :] for half in range(2)], axis=1
            )

        for x in range(PE):
            store_views(xv, x, row_of(src, x), 8)
        xv[:, PE * CELLS :] = jnp.zeros((xv.shape[0], 2 * CELLS), F32)
        edge = jnp.zeros((192, CELLS), F32)
        ya[:, 0:CELLS] = edge
        yb[:, 0:CELLS] = edge
        yb[:, (PE + 1) * CELLS :] = edge
        none = jnp.zeros((64, CELLS), BF16)
        gs[0:64, PE * CELLS : (PE + 1) * CELLS] = none
        gs[128:192, CELLS : 2 * CELLS] = none

        def forward(yy, x):
            return yy[0:64, cols(x)] + yy[64:128, cols(x, 1)] + yy[128:192, cols(x, 2)]

        def backward(yy, x):
            return yy[0:64, cols(x, 2)] + yy[64:128, cols(x, 1)] + yy[128:192, cols(x)]

        def conv_a(x):
            ya[:, cols(x, 1)] = dot_nn(w1[...], xv[:, cols(x)].astype(BF16))

        def hidden_a(x):
            hidden, slope = silu_parts(forward(ya, x))
            s1[:, cols(x)] = slope
            store_views(vv, x, hidden.astype(BF16), 64)

        conv_a(0)
        conv_a(1)
        conv_a(2)
        hidden_a(0)

        def ahead(x):
            done = dot_nn(w2[...], vv[:, cols(x, -1)])
            conv_a(x + 2)
            hidden_a(x)
            yb[:, cols(x)] = done

        for x in range(1, PE):
            ahead(x)
            if 3 <= x < 9:
                extract(x)
            elif 9 <= x < 12:
                backward_weights(x - 9, mid, w2b)
        yb[:, cols(PE)] = dot_nn(w2[...], vv[:, cols(PE - 1)])

        def last(x, carry):
            total, grad_last = carry
            hidden, slope = silu_parts(forward(yb, x))
            hidden = hidden.astype(BF16)
            miss = dot_nn(wl[...], hidden) - row_of(tgt, x)
            total = total + miss * miss
            grad_pred = (miss * grad_scale).astype(BF16)
            grad_last = grad_last + dot_nt(grad_pred, hidden)
            grad = (dot_nn(wlt[...], grad_pred) * slope).astype(BF16)
            store_views(gv, x, grad, 64)
            gs[0:64, cols(x)] = grad
            gs[64:128, cols(x, 1)] = grad
            gs[128:192, cols(x, 2)] = grad
            return total, grad_last

        def back(x, carry):
            done = dot_nn(w2b[...], gv[:, cols(x, -1)])
            carry = last(x, carry)
            ya[:, cols(x)] = done
            return carry

        zero = (jnp.zeros((8, CELLS), F32), jnp.zeros((8, 64), F32))
        carry = last(0, zero)
        for x in range(1, PE):
            carry = back(x, carry)
        total, grad_last = carry
        ya[:, cols(PE)] = dot_nn(w2b[...], gv[:, cols(PE - 1)])
        ya[:, (PE + 1) * CELLS : (PE + 2) * CELLS] = edge

        acc[...] = jnp.zeros(acc.shape, F32)

        def weight_b(i):
            at = slice(2 * i * CELLS, 2 * (i + 1) * CELLS)
            at1 = slice((2 * i + 1) * CELLS, (2 * i + 3) * CELLS)
            more = dot_nt(gs[:, at1], vv[:, at])
            for k in range(2):
                x = 2 * i + k
                gv[0:64, cols(x)] = (backward(ya, x) * s1[:, cols(x)]).astype(BF16)
            acc[...] += more

        for i in range(PE // 2):
            weight_b(i)
        gs[0:64, PE * CELLS : (PE + 1) * CELLS] = none
        g1 = gv[0:64, 0 : PE * CELLS]
        shift = jnp.zeros((64, CELLS), BF16)
        whole = PE * CELLS
        stacked = jnp.concatenate(
            [
                jnp.concatenate([g1[:, CELLS:], shift], axis=1),
                g1,
                jnp.concatenate([shift, g1[:, : whole - CELLS]], axis=1),
            ],
            axis=0,
        )
        grad_first = dot_nt(xv[:, 0:whole].astype(BF16), stacked)

        for i in range(24):
            for j in range(4):
                out[4 * i + j] = acc[8 * i : 8 * i + 8, LANES * j : LANES * (j + 1)]
        for i in range(12):
            out[96 + i] = jnp.concatenate(
                [acc[8 * i : 8 * i + 8, 512:576], acc[8 * i + 96 : 8 * i + 104, 512:576]], axis=1
            )
        for i in range(9):
            out[108 + i] = grad_first[8 * i : 8 * i + 8, 0:LANES]
        for i in range(5):
            j = min(i + 5, 8)
            out[117 + i] = jnp.concatenate(
                [grad_first[8 * i : 8 * i + 8, 128:192], grad_first[8 * j : 8 * j + 8, 128:192]],
                axis=1,
            )
        loss = jnp.sum(total) * (1.0 / (PE**3 * LIVE_ROW))
        corner = lane_of((8, LANES))
        deep = lax.broadcasted_iota(jnp.int32, (8, LANES), 0)
        padded = jnp.concatenate([grad_last, jnp.zeros((8, 64), F32)], axis=1)
        out[122] = jnp.where((deep == 7) & (corner == 64 + dest), loss, padded)
        for i in range(123, 128):
            out[i] = jnp.zeros((8, LANES), F32)


def sum_kernel(shares, out):
    out[...] = jnp.broadcast_to(jnp.sum(shares[...], axis=0, keepdims=True), out.shape)


def unpack_kernel(parts, first, mid, last, loss):
    for dx in range(3):
        for t in range(8):
            i = 8 * dx + t
            for k in range(9):
                if k < 8:
                    block, half = parts[4 * i + k // 2], k % 2
                else:
                    block, half = parts[96 + i % 12], i // 12
                mid[9 * dx + k, 8 * t : 8 * t + 8, :] = block[:, 64 * half : 64 * half + 64]
    for k in range(9):
        tail = parts[117 + k % 5]
        half = k // 5
        head = parts[108 + k]
        by_dx = (head[:, 0:64], head[:, 64:128], tail[:, 64 * half : 64 * half + 64])
        for dx in range(3):
            for c in range(3):
                first[c, 9 * dx + k : 9 * dx + k + 1, :] = by_dx[dx][c : c + 1]
    final = parts[122]
    last[...] = final[0:6, 0:64]
    corner = lane_of((8, LANES))
    deep = lax.broadcasted_iota(jnp.int32, (8, LANES), 0)
    row = lax.axis_index("group") * lax.axis_size("dp") + lax.axis_index("dp")
    mine = (deep == 7) & (corner == 64 + row)
    loss[0] = jnp.sum(jnp.where(mine, final, 0.0))


VMEM = pl.BlockSpec()
HERE = pl.BlockSpec(memory_space=pltpu.VMEM)
AWAY = pl.BlockSpec(memory_space=pltpu.HBM)
SMEM = pl.BlockSpec(memory_space=pltpu.SMEM)


def params(mib):
    return pltpu.CompilerParams(vmem_limit_bytes=mib * 1024 * 1024)


def train_call(table, own, wlo, whi, weights, row_count):
    grad_scale = 2.0 / (PE**3 * row_count * LIVE_ROW)
    whole = PE * CELLS
    height = own.shape[1] + 2 * HALO
    return pl.pallas_call(
        functools.partial(train_kernel, grad_scale),
        out_shape=jax.ShapeDtypeStruct((128, 8, LANES), F32),
        in_specs=[SMEM] + [VMEM] * 6,
        out_specs=VMEM,
        scratch_shapes=[
            pltpu.VMEM((192, 72), BF16),
            pltpu.VMEM((192, 576), BF16),
            pltpu.VMEM((192, 576), BF16),
            pltpu.VMEM((8, 64), BF16),
            pltpu.VMEM((64, 8), BF16),
            pltpu.VMEM((3, 72, 64), F32),
            pltpu.VMEM((3, height, 8, LANES), F32),
            pltpu.VMEM((3, height, 8, LANES), F32),
            pltpu.VMEM((3, height, 8, LANES), F32),
            pltpu.VMEM((9, 8 * PE, LANES), F32),
            pltpu.VMEM((2, 8 * PE, LANES), F32),
            pltpu.VMEM((2, 8 * PE, LANES), F32),
            pltpu.VMEM((72, whole + 2 * CELLS), F32),
            pltpu.VMEM((576, whole), BF16),
            pltpu.VMEM((576, whole), BF16),
            pltpu.VMEM((192, whole + 3 * CELLS), F32),
            pltpu.VMEM((192, whole + 2 * CELLS), F32),
            pltpu.VMEM((64, whole), F32),
            pltpu.VMEM((192, whole + 2 * CELLS), BF16),
            pltpu.VMEM((192, 576), F32),
        ],
        compiler_params=params(60),
        cost_estimate=pl.CostEstimate(flops=10**7, bytes_accessed=6 * 10**7, transcendentals=0),
    )(table, own, wlo, whi, *weights)


def local(
    velocity, conv_first, conv_mid, conv_last, corner_x, corner_z, corner_y, patch_live, patch_dest
):
    row_count = patch_live.shape[0]
    _, count, levels, _ = velocity.shape
    strip = jax.ShapeDtypeStruct((3, levels, LANES), F32)
    up_row = [(i, (i + 1) % row_count) for i in range(row_count)]
    down_row = [(j, i) for i, j in up_row]
    cols_n = lax.axis_size("space")
    up_col = [(i, (i + 1) % cols_n) for i in range(cols_n)]
    down_col = [(j, i) for i, j in up_col]

    table = (patch_live + 2 * corner_x + 16 * corner_z + 1024 * corner_y + 2**18 * patch_dest).T
    rows5 = jax.ShapeDtypeStruct((3, HALO, levels, LANES), F32)
    lo, hi, low_rows, high_rows = pl.pallas_call(
        pack_kernel,
        out_shape=(strip, strip, rows5, rows5),
        in_specs=[VMEM],
        out_specs=(HERE,) * 4,
        compiler_params=params(8),
    )(velocity)
    left = lax.ppermute(hi, "space", up_col)
    right = lax.ppermute(lo, "space", down_col)
    edge = jax.ShapeDtypeStruct((3, HALO, 8, LANES), F32)
    up, down = pl.pallas_call(
        functools.partial(edge_kernel, row_count, count),
        out_shape=(edge, edge),
        in_specs=[SMEM] + [HERE] * 4,
        out_specs=(HERE, HERE),
        compiler_params=params(8),
    )(table, low_rows, high_rows, left, right)
    wlo = lax.ppermute(up, ROWS, up_row)
    whi = lax.ppermute(down, ROWS, down_row)
    face = jax.ShapeDtypeStruct((3, HALO + 1, levels, LANES), F32)
    own, to_up, to_down = pl.pallas_call(
        own_kernel,
        out_shape=(jax.ShapeDtypeStruct((3, count, 8, LANES), F32), face, face),
        in_specs=[SMEM, VMEM, HERE, HERE],
        out_specs=(HERE,) * 3,
        compiler_params=params(12),
    )(table, velocity, left, right)
    weights = (conv_first.transpose(2, 0, 1), conv_mid, conv_last)
    to_up, to_down, wlo, whi = lax.optimization_barrier((to_up, to_down, wlo, whi))
    xlo = lax.ppermute(to_up, ROWS, up_row)
    xhi = lax.ppermute(to_down, ROWS, down_row)
    parts = train_call(table, own, wlo, whi, weights, row_count)

    parts, velocity, xlo, xhi = lax.optimization_barrier((parts, velocity, xlo, xhi))
    shares = lax.all_to_all(parts, EVERY, 0, 0, tiled=True)
    wide = 2 * LANES
    height = count + 2 * HALO
    nxt, wide_next = pl.pallas_call(
        solver_kernel,
        out_shape=(
            jax.ShapeDtypeStruct(velocity.shape, F32),
            jax.ShapeDtypeStruct((3, height - 4, levels, wide), F32),
        ),
        in_specs=[VMEM] + [AWAY] * 4,
        out_specs=(VMEM, VMEM),
        scratch_shapes=[
            pltpu.VMEM((3, height, levels, wide), F32),
            pltpu.VMEM((3, height - 2, levels, wide), F32),
            pltpu.VMEM(xlo.shape, F32),
            pltpu.VMEM(xhi.shape, F32),
            pltpu.VMEM(left.shape, F32),
            pltpu.VMEM(right.shape, F32),
            pltpu.SemaphoreType.DMA((4,)),
        ],
        compiler_params=params(60),
        cost_estimate=pl.CostEstimate(flops=10**7, bytes_accessed=4 * 10**7, transcendentals=0),
    )(velocity, xlo, xhi, left, right)
    shares, wide_next = lax.optimization_barrier((shares, wide_next))
    filt, stress = pl.pallas_call(
        filter_kernel,
        out_shape=(
            jax.ShapeDtypeStruct(velocity.shape, F32),
            jax.ShapeDtypeStruct((6,) + velocity.shape[1:], F32),
        ),
        in_specs=[VMEM],
        out_specs=(VMEM, VMEM),
        scratch_shapes=[pltpu.VMEM((2, count * levels, 6 * LANES), BF16)],
        compiler_params=params(24),
        cost_estimate=pl.CostEstimate(flops=10**7, bytes_accessed=4 * 10**7, transcendentals=0),
    )(wide_next)
    mine = pl.pallas_call(
        sum_kernel,
        out_shape=jax.ShapeDtypeStruct(parts.shape, F32),
        in_specs=[VMEM],
        out_specs=VMEM,
        compiler_params=params(8),
    )(shares)
    summed = lax.all_to_all(mine, EVERY, 0, 0, tiled=True)
    grad_first, grad_mid, grad_last, loss = pl.pallas_call(
        unpack_kernel,
        out_shape=(
            jax.ShapeDtypeStruct((3, 27, 64), F32),
            jax.ShapeDtypeStruct((27, 64, 64), F32),
            jax.ShapeDtypeStruct((6, 64), F32),
            jax.ShapeDtypeStruct((1,), F32),
        ),
        in_specs=[HERE],
        out_specs=(VMEM, VMEM, VMEM, SMEM),
        compiler_params=params(8),
    )(summed)
    return (nxt, filt, stress, grad_first.transpose(1, 2, 0), grad_mid, grad_last, loss)


def solution(mesh):
    block = P(None, ("group", "dp"), None, "space")
    in_specs = (block,) + (P(),) * 8
    out_specs = (block, block, block, P(), P(), P(), P(("group", "dp")))
    return jax.shard_map(local, mesh=mesh, in_specs=in_specs, out_specs=out_specs, check_vma=False)
```
